32 devices in a mesh: dp: 4 (over y, x), ctx: 8 (over z, core).
Axes of the slice: x: 2, y: 2, z: 4, core: 2. Of those that a mesh axis runs over, the one named last changes fastest.
Arguments:
- tokens: bfloat16 [4, 2048, 640], P('dp', 'ctx'), may hold values from -6 to 6
- doc_starts: int32 [4, 4], P('dp'), may hold values from 0 to 2047, as said below
- attn_gain: bfloat16 [640], P('dp'), may hold values from 0.099609375 to 1.8984375
- query_gain: bfloat16 [256], P('dp'), may hold values from 0.099609375 to 1.8984375
- key_gain: bfloat16 [256], P('dp'), may hold values from 0.099609375 to 1.8984375
- post_attn_gain: bfloat16 [640], P('dp'), may hold values from 0.099609375 to 1.8984375
- ffw_gain: bfloat16 [640], P('dp'), may hold values from 0.099609375 to 1.8984375
- post_ffw_gain: bfloat16 [640], P('dp'), may hold values from 0.099609375 to 1.8984375
- w_query: bfloat16 [640, 1024], P(None, 'dp'), may hold values from -0.25 to 0.25
- w_key: bfloat16 [640, 256], P(None, 'dp'), may hold values from -0.25 to 0.25
- w_value: bfloat16 [640, 256], P(None, 'dp'), may hold values from -0.25 to 0.25
- w_out: bfloat16 [1024, 640], P('dp'), may hold values from -0.1875 to 0.1875
- w_gate: bfloat16 [640, 2048], P(None, 'dp'), may hold values from -0.25 to 0.25
- w_up: bfloat16 [640, 2048], P(None, 'dp'), may hold values from -0.25 to 0.25
- w_down: bfloat16 [2048, 640], P('dp'), may hold values from -0.125 to 0.125
- cotangent: bfloat16 [4, 2048, 640], P('dp', 'ctx'), may hold values from -6 to 6
Outputs:
- output: bfloat16 [4, 2048, 640], P('dp', 'ctx')
- grad_tokens: bfloat16 [4, 2048, 640], P('dp', 'ctx')
- grad_attn_gain: float32 [640], P('dp')
- grad_query_gain: float32 [256], P('dp')
- grad_key_gain: float32 [256], P('dp')
- grad_post_attn_gain: float32 [640], P('dp')
- grad_ffw_gain: float32 [640], P('dp')
- grad_post_ffw_gain: float32 [640], P('dp')
- grad_w_query: float32 [640, 1024], P(None, 'dp')
- grad_w_key: float32 [640, 256], P(None, 'dp')
- grad_w_value: float32 [640, 256], P(None, 'dp')
- grad_w_out: float32 [1024, 640], P('dp')
- grad_w_gate: float32 [640, 2048], P(None, 'dp')
- grad_w_up: float32 [640, 2048], P(None, 'dp')
- grad_w_down: float32 [2048, 640], P('dp')
The draws below stay inside these ranges and needn't reach their ends.
Inputs may be any that keep to these rules, and one draw needn't show every extreme that they name: `doc_starts`: per sequence: the first start is 0, starts rise strictly, and one document begins within the first 128 tokens and ends within the last 128 tokens.
All inputs are finite; a program needn't handle non-finite values.
Results may differ from the reference program's by a relative error of at most 0.023.
Values may be sent and summed in bfloat16 or wider, within the bound.
A program may use at most 192 MiB of HBM per device.

```python
import math
import jax
import jax.numpy as jnp
from jax import lax

D = 640
HEADS = 4
HEAD = 256
FF = 2048
TOK_DEV = 256
LENGTH = 2048
SEQS = 4
N_CTX = 8


def draw_doc_starts(key, part):
    key = jax.random.fold_in(key, 7)
    half_size = TOK_DEV // 2
    length = TOK_DEV * N_CTX
    subkeys = jax.random.split(key, 5)
    shape = (SEQS,)
    front = jax.random.randint(subkeys[0], shape, 1, 3)
    early_one = jax.random.randint(subkeys[1], shape, 1, half_size // 2)
    early_two = jax.random.randint(subkeys[2], shape, half_size // 2, half_size)
    late_one = length - half_size + jax.random.randint(subkeys[3], shape, 0, half_size // 2)
    late_two = length - half_size + jax.random.randint(subkeys[4], shape, half_size // 2, half_size)
    anchor = jnp.zeros(shape, jnp.int32)
    one_front = jnp.stack([anchor, early_one, late_one, late_two], axis=1)
    two_front = jnp.stack([anchor, early_one, early_two, late_one], axis=1)
    return jnp.where(front[:, None] == 1, one_front, two_front).astype(jnp.int32)


def levels(rng, shape, cuts, least, high):
    level, own = 1.0, jax.random.fold_in(rng, 6)
    for position, blocks in cuts:
        heights = jnp.exp(jax.random.uniform(jax.random.fold_in(own, position), (blocks,), jnp.float32, least / len(cuts), high / len(cuts)))
        level = level * jnp.repeat(heights, shape[position] // blocks).reshape([-1 if axis == position else 1 for axis in range(len(shape))])
    return level


def gaussian(own_key, extent, scale, limit, shards=(), kind=jnp.bfloat16):
    drawn = jax.random.normal(own_key, extent, jnp.float32) * scale
    if len(shards) > 0:
        drawn = levels(own_key, extent, shards, -0.22, 0.18) * drawn
    return jnp.clip(drawn, min=-limit, max=limit).astype(kind)


def setup_inputs(seed: int = 0) -> dict:
    key_of = jax.random.split(jax.random.key(seed), 17)
    return {
        "tokens": gaussian(key_of[0], (SEQS, LENGTH, D), 1.0, 6.0, ((0, 4), (1, 8))),
        "doc_starts": draw_doc_starts(jax.random.fold_in(key_of[16], 71), 0),
        "attn_gain": jnp.clip(1.0 + 0.18 * jax.random.normal(key_of[2], (D,), jnp.float32), 0.099609375, 1.8984375).astype(jnp.bfloat16),
        "query_gain": jnp.clip(1.0 + 0.18 * jax.random.normal(key_of[3], (HEAD,), jnp.float32), 0.099609375, 1.8984375).astype(jnp.bfloat16),
        "key_gain": jnp.clip(1.0 + 0.18 * jax.random.normal(key_of[4], (HEAD,), jnp.float32), 0.099609375, 1.8984375).astype(jnp.bfloat16),
        "post_attn_gain": jnp.clip(1.0 + 0.18 * jax.random.normal(key_of[5], (D,), jnp.float32), 0.099609375, 1.8984375).astype(jnp.bfloat16),
        "ffw_gain": jnp.clip(1.0 + 0.18 * jax.random.normal(key_of[6], (D,), jnp.float32), 0.099609375, 1.8984375).astype(jnp.bfloat16),
        "post_ffw_gain": jnp.clip(1.0 + 0.18 * jax.random.normal(key_of[7], (D,), jnp.float32), 0.099609375, 1.8984375).astype(jnp.bfloat16),
        "w_query": gaussian(key_of[8], (D, HEADS * HEAD), D ** -0.5, 0.25, ((1, 4),)),
        "w_key": gaussian(key_of[9], (D, HEAD), D ** -0.5, 0.25, ((1, 4),)),
        "w_value": gaussian(key_of[10], (D, HEAD), D ** -0.5, 0.25, ((1, 4),)),
        "w_out": gaussian(key_of[11], (HEADS * HEAD, D), (HEADS * HEAD) ** -0.5, 0.1875, ((0, 4),)),
        "w_gate": gaussian(key_of[12], (D, FF), D ** -0.5, 0.25, ((1, 4),)),
        "w_up": gaussian(key_of[13], (D, FF), D ** -0.5, 0.25, ((1, 4),)),
        "w_down": gaussian(key_of[14], (FF, D), FF ** -0.5, 0.125, ((0, 4),)),
        "cotangent": gaussian(key_of[15], (SEQS, LENGTH, D), 1.0, 6.0, ((0, 4), (1, 8))),
    }


@jax.custom_vjp
def low(v):
    return lax.optimization_barrier(v.astype(jnp.bfloat16)).astype(jnp.float32)

@jax.custom_vjp
def low_back(v):
    return v

def low_keep(v):
    return (low(v), None)

def low_pass(kept, grad):
    return (grad,)

def back_keep(v):
    return (v, None)

def back_low(kept, grad):
    return (low(grad),)
low.defvjp(low_keep, low_pass)
low_back.defvjp(back_keep, back_low)
EPSILON = 1e-06
THETA = 1000000.0
NEGATIVE = -1e+30

def matmul(left, right):
    return jnp.dot(left, right, precision=lax.Precision.HIGHEST, preferred_element_type=jnp.float32)

def rms_norm(value, gain_vec):
    inverse = lax.rsqrt(lax.optimization_barrier(jnp.mean(value * value, axis=-1, keepdims=True)) + EPSILON)
    return value * inverse * gain_vec

def frequencies(head_size):
    half_size = head_size // 2
    return jnp.exp(jnp.arange(half_size, dtype=jnp.float32) * (-2.0 * math.log(THETA) / head_size))

def rotate(value, cosine, sine_part):
    half_size = value.shape[-1] // 2
    leading = value[..., :half_size]
    trailing = value[..., half_size:]
    return jnp.concatenate([leading * cosine - trailing * sine_part, trailing * cosine + leading * sine_part], axis=-1)

def doc_info(starts, positions):
    below = starts[None, :] <= positions[:, None]
    doc_ids = lax.optimization_barrier(jnp.sum(below.astype(jnp.int32), axis=1))
    begins = lax.optimization_barrier(jnp.max(jnp.where(below, starts[None, :], 0), axis=1))
    return (doc_ids, positions - begins)

def attention(query, key_rows, value_rows, doc_ids):
    length = query.shape[0]
    block = math.gcd(length, 512)
    count = length // block
    factor = 1.0 / math.sqrt(HEAD)
    key_pos = jnp.arange(length, dtype=jnp.int32)
    query_blocks = query.reshape(count, block, HEADS, HEAD)

    def one_block(pair):
        q_block, block_index = pair
        q_pos = block_index * block + jnp.arange(block, dtype=jnp.int32)
        q_doc = lax.dynamic_slice_in_dim(doc_ids, block_index * block, block)
        scores = jnp.einsum('qhe,ke->hqk', q_block, key_rows, precision=lax.Precision.HIGHEST)
        scores = low_back(scores * factor)
        allowed = (key_pos[None, :] <= q_pos[:, None]) & (doc_ids[None, :] == q_doc[:, None])
        scores = jnp.where(allowed[None], scores, NEGATIVE)
        peak = lax.optimization_barrier(jnp.max(scores, axis=-1, keepdims=True))
        weights = jnp.exp(scores - peak)
        probs = low(weights / lax.optimization_barrier(jnp.sum(weights, axis=-1, keepdims=True)))
        return jnp.einsum('hqk,ke->qhe', probs, value_rows, precision=lax.Precision.HIGHEST)
    result = lax.map(jax.checkpoint(one_block), (query_blocks, jnp.arange(count, dtype=jnp.int32)))
    return result.reshape(length, HEADS * HEAD)

def layer(stream, starts, params):
    g_attn, g_query, g_key, g_post, g_ffw, g_pffw, wq_full, wk_full, wv_full, wo_full, wg_full, wu_full, wd_full = params
    length = stream.shape[0]
    positions = jnp.arange(length, dtype=jnp.int32)
    doc_ids, offsets = doc_info(starts, positions)
    angles = offsets.astype(jnp.float32)[:, None] * frequencies(HEAD)[None, :]
    cosine = jnp.cos(angles)
    sine_part = jnp.sin(angles)
    normed = low(rms_norm(stream, g_attn))
    query = low_back(matmul(normed, wq_full)).reshape(length, HEADS, HEAD)
    key_rows = low_back(matmul(normed, wk_full))
    value_rows = low(low_back(matmul(normed, wv_full)))
    query = low(rotate(rms_norm(query, g_query), cosine[:, None, :], sine_part[:, None, :]))
    key_rows = low(rotate(rms_norm(key_rows, g_key), cosine, sine_part))
    attended = low(low_back(attention(query, key_rows, value_rows, doc_ids)))
    branch = low_back(matmul(attended, wo_full))
    hidden_state = stream + rms_norm(branch, g_post)
    ffw_in = low(rms_norm(hidden_state, g_ffw))
    gate_act = low_back(matmul(ffw_in, wg_full))
    up_act = low_back(matmul(ffw_in, wu_full))
    inner_act = low(jax.nn.gelu(gate_act, approximate=True) * up_act)
    down_out = low_back(matmul(inner_act, wd_full))
    return hidden_state + rms_norm(down_out, g_pffw)

def reference(tokens, doc_starts, attn_gain, query_gain, key_gain, post_attn_gain, ffw_gain, post_ffw_gain, w_query, w_key, w_value, w_out, w_gate, w_up, w_down, cotangent):
    params = tuple((item.astype(jnp.float32) for item in (attn_gain, query_gain, key_gain, post_attn_gain, ffw_gain, post_ffw_gain, w_query, w_key, w_value, w_out, w_gate, w_up, w_down)))
    stream = tokens.astype(jnp.float32)

    def whole(stream_in, *weights):
        return lax.map(lambda pair: layer(pair[0], pair[1], weights), (stream_in, doc_starts))
    result, pullback = jax.vjp(whole, stream, *params)
    grads = pullback(cotangent.astype(jnp.float32))
    return (result.astype(jnp.bfloat16), grads[0].astype(jnp.bfloat16), grads[1], grads[2], grads[3], grads[4], grads[5], grads[6], grads[7], grads[8], grads[9], grads[10], grads[11], grads[12], grads[13])
```

```python
import functools
import math

import jax
import jax.numpy as jnp
from jax import lax
from jax.sharding import PartitionSpec as P

EPSILON = 1e-06
THETA = 1000000.0
NEGATIVE = -1e30


def frequencies(head_size):
    half_size = head_size // 2
    return jnp.exp(jnp.arange(half_size, dtype=jnp.float32) * (-2.0 * math.log(THETA) / head_size))


def rotate(value, cosine, sine_part):
    half_size = value.shape[-1] // 2
    leading = value[..., :half_size]
    trailing = value[..., half_size:]
    return jnp.concatenate(
        [leading * cosine - trailing * sine_part, trailing * cosine + leading * sine_part], axis=-1
    )


def doc_info(starts, positions):
    below = starts[None, :] <= positions[:, None]
    doc_ids = jnp.sum(below.astype(jnp.int32), axis=1)
    begins = jnp.max(jnp.where(below, starts[None, :], 0), axis=1)
    return (doc_ids, positions - begins)


def norm_forward(value, gain_vec):
    inverse = lax.rsqrt(jnp.mean(value * value, axis=-1, keepdims=True) + EPSILON)
    return (value * inverse * gain_vec, inverse)


def norm_backward(value, inverse, gain_vec, grad_in):
    scaled = grad_in * gain_vec
    inner_mean = jnp.mean(scaled * value, axis=-1, keepdims=True)
    grad_value = inverse * (scaled - value * inverse * inverse * inner_mean)
    grad_gain = jnp.sum((grad_in * value * inverse).reshape(-1, value.shape[-1]), axis=0)
    return (grad_value, grad_gain)


def product(left, right, form):
    return jnp.einsum(form, left, right, preferred_element_type=jnp.float32)


def fold_keys(state_now, piece, query, q_pos, q_doc, starts):
    key_rows, value_rows = piece
    count = key_rows.shape[0]
    block = math.gcd(count, 1024)
    factor = 1.0 / math.sqrt(query.shape[-1])

    def fold_step(state_in, block_index):
        key_block = lax.dynamic_slice_in_dim(key_rows, block_index * block, block, 0)
        value_block = lax.dynamic_slice_in_dim(value_rows, block_index * block, block, 0)
        key_pos = block_index * block + jnp.arange(block, dtype=jnp.int32)
        key_doc, unused_offsets = doc_info(starts, key_pos)

        def fold_compute(state_old):
            peak_old, denominator, accumulated = state_old
            scores = product(query, key_block, "qhe,ke->hqk") * factor
            allowed = (key_pos[None, :] <= q_pos[:, None]) & (key_doc[None, :] == q_doc[:, None])
            scores = jnp.where(allowed[None], scores, NEGATIVE)
            peak_new = jnp.maximum(peak_old, jnp.max(scores, axis=-1))
            weights = jnp.where(allowed[None], jnp.exp(scores - peak_new[..., None]), 0.0)
            shrink = jnp.exp(peak_old - peak_new)
            denominator = denominator * shrink + jnp.sum(weights, axis=-1)
            accumulated = accumulated * shrink[..., None] + product(
                weights.astype(jnp.bfloat16), value_block, "hqk,ke->hqe"
            )
            return (peak_new, denominator, accumulated)

        skipped = key_pos[0] > q_pos[-1]
        return (lax.cond(skipped, lambda state_old: state_old, fold_compute, state_in), None)

    state_out, unused_stack = lax.scan(
        fold_step, state_now, jnp.arange(count // block, dtype=jnp.int32)
    )
    return state_out


def back_keys(
    key_rows, value_rows, begin_at, query, d_heads, log_total, delta, q_pos, q_doc, starts
):
    count = key_rows.shape[0]
    block = math.gcd(count, 1024)
    factor = 1.0 / math.sqrt(query.shape[-1])
    width = key_rows.shape[1]

    def back_step(d_query, block_index):
        key_block = lax.dynamic_slice_in_dim(key_rows, block_index * block, block, 0)
        value_block = lax.dynamic_slice_in_dim(value_rows, block_index * block, block, 0)
        key_pos = begin_at + block_index * block + jnp.arange(block, dtype=jnp.int32)
        key_doc, unused_offsets = doc_info(starts, key_pos)

        def back_compute(d_old):
            scores = product(query, key_block, "qhe,ke->hqk") * factor
            allowed = (key_pos[None, :] <= q_pos[:, None]) & (key_doc[None, :] == q_doc[:, None])
            scores = jnp.where(allowed[None], scores, NEGATIVE)
            probs = jnp.where(allowed[None], jnp.exp(scores - log_total[..., None]), 0.0)
            d_probs = product(d_heads, value_block, "hqe,ke->hqk")
            d_scores = (probs * (d_probs - delta[..., None])).astype(jnp.bfloat16)
            d_new = d_old + product(d_scores, key_block, "hqk,ke->qhe") * factor
            d_values = product(probs.astype(jnp.bfloat16), d_heads, "hqk,hqe->ke")
            d_keys = product(d_scores, query, "hqk,qhe->ke") * factor
            return (d_new, (d_keys, d_values))

        def skip(d_old):
            empty = jnp.zeros((block, width), jnp.float32)
            return (d_old, (empty, empty))

        return lax.cond(key_pos[0] > q_pos[-1], skip, back_compute, d_query)

    d_query, stacked = lax.scan(
        back_step, jnp.zeros(query.shape, jnp.float32), jnp.arange(count // block, dtype=jnp.int32)
    )
    d_keys, d_values = stacked
    return (d_query, d_keys.reshape(count, width), d_values.reshape(count, width))


class Links:
    def __init__(self, n_dp, n_ctx):
        self.n_dp = n_dp
        self.n_ctx = n_ctx
        self.n_chip = n_ctx // 2
        self.dp = lax.axis_index("dp")
        ctx = lax.axis_index("ctx")
        self.core = lax.rem(ctx, 2)
        self.chip = ctx // 2
        self.near = jnp.where(self.core == 0, 1, 2)
        self.far = 3 - self.near

    def send(self, value, target):
        pairs = []
        for d in range(self.n_dp):
            for c in range(self.n_ctx):
                to_d, to_c = target(d, c)
                pairs.append((d * self.n_ctx + c, to_d * self.n_ctx + to_c))
        return lax.ppermute(value, ("dp", "ctx"), pairs)

    def to_core(self, value):
        return self.send(value, lambda d, c: (d, c ^ 1))

    def to_near(self, value):
        return self.send(value, lambda d, c: (d ^ (1 + c % 2), c))

    def to_far(self, value):
        return self.send(value, lambda d, c: (d ^ (2 - c % 2), c))

    def to_chip(self, value, bit):
        return self.send(value, lambda d, c: (d, c ^ (2 << bit)))

    def in_order(self, flag, mine, other, axis):
        return jnp.where(
            flag == 0,
            jnp.concatenate([mine, other], axis=axis),
            jnp.concatenate([other, mine], axis=axis),
        )

    def gather(self, piece):
        near = self.to_near(piece)
        far = self.to_far(piece)
        both = self.to_far(near)
        whole = jnp.zeros((self.n_dp,) + piece.shape, piece.dtype)
        for block, index in (
            (piece, self.dp),
            (near, self.dp ^ self.near),
            (far, self.dp ^ self.far),
            (both, self.dp ^ 3),
        ):
            whole = lax.dynamic_update_slice_in_dim(whole, block[None], index, 0)
        return whole

    def reduce(self, halves):
        low = jnp.bfloat16

        def pick(value, index):
            return lax.dynamic_index_in_dim(value, index, 0, keepdims=False)

        received = self.to_core(pick(halves, 1 - self.core).astype(low))
        mine = pick(halves, self.core) + received.astype(jnp.float32)
        out_pair = jnp.stack(
            [pick(mine, self.dp ^ self.far), pick(mine, self.dp ^ 3)]
        ).astype(low)
        got_pair = self.to_far(out_pair).astype(jnp.float32)
        keep = pick(mine, self.dp) + got_pair[0]
        give = pick(mine, self.dp ^ self.near) + got_pair[1]
        total = keep + self.to_near(give.astype(low)).astype(jnp.float32)
        bits = self.n_chip.bit_length() - 1
        for bit in range(bits):
            flag = (self.chip >> bit) & 1
            size = total.shape[0] // 2
            give = lax.dynamic_slice_in_dim(total, (1 - flag) * size, size, 0)
            keep = lax.dynamic_slice_in_dim(total, flag * size, size, 0)
            total = keep + self.to_chip(give.astype(low), bit).astype(jnp.float32)
        total = total.astype(low)
        for bit in reversed(range(bits)):
            flag = (self.chip >> bit) & 1
            total = self.in_order(flag, total, self.to_chip(total, bit), 0)
        return self.in_order(self.core, total[None], self.to_core(total)[None], 0)


GAIN_ROWS = 32


def local(
    tokens,
    doc_starts,
    attn_gain,
    query_gain,
    key_gain,
    post_attn_gain,
    ffw_gain,
    post_ffw_gain,
    w_query,
    w_key,
    w_value,
    w_out,
    w_gate,
    w_up,
    w_down,
    cotangent,
    n_dp,
    n_ctx,
):
    links = Links(n_dp, n_ctx)
    f32 = jnp.float32
    low = jnp.bfloat16
    width = tokens.shape[2]
    gains = (attn_gain, query_gain, key_gain, post_attn_gain, ffw_gain, post_ffw_gain)
    gain_sizes = [item.shape[0] for item in gains]
    cols_q, cols_k = w_query.shape[1], w_key.shape[1]
    cols_qkv = cols_q + 2 * cols_k
    cols_ff = w_gate.shape[1]
    half = width // 2
    gain_used = -(-sum(gain_sizes) // cols_qkv)
    gain_flat = jnp.concatenate(gains)
    gain_flat = jnp.pad(gain_flat, (0, GAIN_ROWS * cols_qkv - gain_flat.shape[0]))
    gain_block = gain_flat.reshape(GAIN_ROWS, cols_qkv)

    def core_rows(value, which):
        size = value.shape[0] // 2
        return lax.dynamic_slice_in_dim(value, which * size, size, 0)

    own_qkv = core_rows(jnp.concatenate([w_query, w_key, w_value], axis=1), links.core)
    half_qkv = links.gather(jnp.concatenate([own_qkv, gain_block], axis=0))
    half_out = links.gather(core_rows(w_out, links.core))
    half_gu = links.gather(core_rows(jnp.concatenate([w_gate, w_up], axis=1), links.core))
    half_down = links.gather(core_rows(w_down, links.core))

    gain_all = half_qkv[:, half : half + gain_used].reshape(n_dp, gain_used * cols_qkv)
    gain_list = []
    at = 0
    for size in gain_sizes:
        gain_list.append(gain_all[:, at : at + size].reshape(-1).astype(f32))
        at += size
    g_attn, g_query, g_key, g_post, g_ffw, g_pffw = gain_list

    def columns(value):
        value = value[:, :half]
        value = jnp.transpose(value, (1, 0, 2)).reshape(half, -1)
        return links.in_order(links.core, value, links.to_core(value), 0)

    def rows(value):
        other = links.to_core(value)
        value = links.in_order(links.core, value[:, None], other[:, None], 1)
        return value.reshape(-1, value.shape[-1])

    w_qkv_full = columns(half_qkv)
    wo_full = rows(half_out)
    w_gu_full = columns(half_gu)
    wd_full = rows(half_down)

    row_count = tokens.shape[1]
    head_size = g_query.shape[0]
    head_count = n_dp * cols_q // head_size
    starts = doc_starts[0]
    positions = lax.axis_index("ctx") * row_count + jnp.arange(row_count, dtype=jnp.int32)
    doc_ids, offsets = doc_info(starts, positions)
    angles = offsets.astype(jnp.float32)[:, None] * frequencies(head_size)[None, :]
    cosine = jnp.cos(angles)
    sine_part = jnp.sin(angles)
    stream = tokens[0].astype(jnp.float32)
    normed, attn_inverse = norm_forward(stream, g_attn)
    normed_low = normed.astype(jnp.bfloat16)
    qkv = product(normed_low, w_qkv_full, "td,da->ta").reshape(row_count, n_dp, cols_qkv)
    query_raw = qkv[:, :, :cols_q].reshape(row_count, head_count, head_size)
    key_raw = qkv[:, :, cols_q : cols_q + cols_k].reshape(row_count, head_size)
    value_low = qkv[:, :, cols_q + cols_k :].reshape(row_count, head_size).astype(jnp.bfloat16)
    query_normed, query_inverse = norm_forward(query_raw, g_query)
    key_normed, key_inverse = norm_forward(key_raw, g_key)
    query_low = rotate(query_normed, cosine[:, None, :], sine_part[:, None, :]).astype(jnp.bfloat16)
    key_low = rotate(key_normed, cosine, sine_part).astype(jnp.bfloat16)
    initial = (
        jnp.full((head_count, row_count), NEGATIVE, jnp.float32),
        jnp.zeros((head_count, row_count), jnp.float32),
        jnp.zeros((head_count, row_count, head_size), jnp.float32),
    )
    key_value = lax.all_gather(
        jnp.concatenate([key_low, value_low], axis=1), "ctx", axis=0, tiled=True
    )
    key_whole = key_value[:, :head_size]
    value_whole = key_value[:, head_size:]
    peak, denominator, accumulated = fold_keys(
        initial, (key_whole, value_whole), query_low, positions, doc_ids, starts
    )
    log_total = peak + jnp.log(denominator)
    attended = jnp.transpose(accumulated / denominator[..., None], (1, 0, 2)).reshape(
        row_count, head_count * head_size
    )
    attended_low = attended.astype(jnp.bfloat16)
    branch = product(attended_low, wo_full, "ta,ad->td")
    post_branch, post_inverse = norm_forward(branch, g_post)
    hidden_state = stream + post_branch
    ffw_normed, ffw_inverse = norm_forward(hidden_state, g_ffw)
    ffw_low = ffw_normed.astype(jnp.bfloat16)
    gate_up = product(ffw_low, w_gu_full, "td,df->tf").reshape(row_count, n_dp, 2 * cols_ff)
    gate_act = gate_up[:, :, :cols_ff].reshape(row_count, -1)
    up_act = gate_up[:, :, cols_ff:].reshape(row_count, -1)
    inner_act, inner_back = jax.vjp(
        lambda left, right: jax.nn.gelu(left, approximate=True) * right, gate_act, up_act
    )
    inner_low = inner_act.astype(jnp.bfloat16)
    down_out = product(inner_low, wd_full, "tf,fd->td")
    ffw_branch, down_inverse = norm_forward(down_out, g_pffw)
    output = (hidden_state + ffw_branch).astype(jnp.bfloat16)
    grad_output = cotangent[0].astype(jnp.float32)
    d_down, dg_pffw = norm_backward(down_out, down_inverse, g_pffw, grad_output)
    d_down_low = d_down.astype(jnp.bfloat16)
    dw_down = product(inner_low, d_down_low, "tf,td->fd")
    d_inner = product(d_down_low, wd_full, "td,fd->tf")
    d_gate, d_up = inner_back(d_inner)
    d_gate_low = d_gate.astype(jnp.bfloat16)
    d_up_low = d_up.astype(jnp.bfloat16)
    d_gate_up = jnp.concatenate(
        [d_gate_low.reshape(row_count, n_dp, cols_ff), d_up_low.reshape(row_count, n_dp, cols_ff)],
        axis=2,
    ).reshape(row_count, -1)
    dw_gu = product(ffw_low, d_gate_up, "td,tf->df")
    d_ffw_in = product(d_gate_up, w_gu_full, "tf,df->td")
    d_hidden_part, dg_ffw = norm_backward(hidden_state, ffw_inverse, g_ffw, d_ffw_in)
    d_hidden = grad_output + d_hidden_part
    d_branch, dg_post = norm_backward(branch, post_inverse, g_post, d_hidden)
    d_branch_low = d_branch.astype(jnp.bfloat16)
    dw_out = product(attended_low, d_branch_low, "ta,td->ad")
    d_attended = (
        product(d_branch_low, wo_full, "td,ad->ta")
        .astype(jnp.bfloat16)
        .reshape(row_count, head_count, head_size)
    )
    delta = jnp.transpose(
        jnp.sum(
            d_attended.astype(jnp.float32) * attended.reshape(row_count, head_count, head_size),
            axis=-1,
        ),
        (1, 0),
    )
    d_heads = jnp.transpose(d_attended, (1, 0, 2))
    d_query, d_key_all, d_value_all = back_keys(
        key_whole, value_whole, 0, query_low, d_heads, log_total, delta, positions, doc_ids, starts
    )
    d_kv_local = lax.psum_scatter(
        jnp.concatenate([d_key_all, d_value_all], axis=1).astype(low),
        "ctx",
        scatter_dimension=0,
        tiled=True,
    ).astype(f32)
    d_key_local = d_kv_local[:, :head_size]
    d_value_local = d_kv_local[:, head_size:]
    d_value_low = d_value_local.astype(jnp.bfloat16)
    d_key_normed = rotate(d_key_local, cosine, -sine_part)
    d_key_raw, dg_key = norm_backward(key_raw, key_inverse, g_key, d_key_normed)
    d_key_low = d_key_raw.astype(jnp.bfloat16)
    d_query_normed = rotate(d_query, cosine[:, None, :], -sine_part[:, None, :])
    d_query_raw, dg_query = norm_backward(query_raw, query_inverse, g_query, d_query_normed)
    d_query_low = d_query_raw.reshape(row_count, head_count * head_size).astype(jnp.bfloat16)
    d_qkv_low = jnp.concatenate(
        [
            d_query_low.reshape(row_count, n_dp, cols_q),
            d_key_low.reshape(row_count, n_dp, cols_k),
            d_value_low.reshape(row_count, n_dp, cols_k),
        ],
        axis=2,
    ).reshape(row_count, -1)
    dw_qkv = product(normed_low, d_qkv_low, "td,ta->da")
    d_normed = product(d_qkv_low, w_qkv_full, "ta,da->td")
    d_stream_part, dg_attn = norm_backward(stream, attn_inverse, g_attn, d_normed)
    grad_tokens = (d_hidden + d_stream_part).astype(jnp.bfloat16)

    def split_columns(value):
        value = value.reshape(2, half, n_dp, -1)
        return jnp.transpose(value, (0, 2, 1, 3))

    def split_rows(value):
        return jnp.transpose(value.reshape(n_dp, 2, -1, width), (1, 0, 2, 3))

    gain_grads = jnp.concatenate(
        [item.reshape(n_dp, -1) for item in (dg_attn, dg_query, dg_key, dg_post, dg_ffw, dg_pffw)],
        axis=1,
    )
    gain_grads = jnp.pad(gain_grads, ((0, 0), (0, GAIN_ROWS * cols_qkv - gain_grads.shape[1])))
    gain_grads = gain_grads.reshape(1, n_dp, GAIN_ROWS, cols_qkv)
    gain_grads = jnp.broadcast_to(gain_grads, (2,) + gain_grads.shape[1:])

    t_down = links.reduce(split_rows(dw_down)).reshape(-1, width).astype(f32)
    t_gu = links.reduce(split_columns(dw_gu)).reshape(width, -1).astype(f32)
    t_out = links.reduce(split_rows(dw_out)).reshape(-1, width).astype(f32)
    t_qkv = links.reduce(jnp.concatenate([split_columns(dw_qkv), gain_grads], axis=2))
    t_gain = t_qkv[0, half : half + gain_used].reshape(-1).astype(f32)
    t_qkv = t_qkv[:, :half].reshape(width, -1).astype(f32)
    gain_out = []
    at = 0
    for size in gain_sizes:
        gain_out.append(t_gain[at : at + size])
        at += size
    return (
        (output[None], grad_tokens[None])
        + tuple(gain_out)
        + (
            t_qkv[:, :cols_q],
            t_qkv[:, cols_q : cols_q + cols_k],
            t_qkv[:, cols_q + cols_k :],
            t_out,
            t_gu[:, :cols_ff],
            t_gu[:, cols_ff:],
            t_down,
        )
    )


def solution(mesh):
    placed = (
        P("dp", "ctx", None),
        P("dp", None),
        P("dp"),
        P("dp"),
        P("dp"),
        P("dp"),
        P("dp"),
        P("dp"),
        P(None, "dp"),
        P(None, "dp"),
        P(None, "dp"),
        P("dp", None),
        P(None, "dp"),
        P(None, "dp"),
        P("dp", None),
        P("dp", "ctx", None),
    )
    return jax.shard_map(
        functools.partial(local, n_dp=mesh.shape["dp"], n_ctx=mesh.shape["ctx"]),
        mesh=mesh,
        in_specs=placed,
        out_specs=(
            P("dp", "ctx", None),
            P("dp", "ctx", None),
            P("dp"),
            P("dp"),
            P("dp"),
            P("dp"),
            P("dp"),
            P("dp"),
            P(None, "dp"),
            P(None, "dp"),
            P(None, "dp"),
            P("dp", None),
            P(None, "dp"),
            P(None, "dp"),
            P("dp", None),
        ),
        check_vma=False,
    )
```

```python
import functools
import math

import jax
import jax.numpy as jnp
from jax import lax
from jax.sharding import PartitionSpec as P

EPSILON = 1e-06
THETA = 1000000.0
NEGATIVE = -1e30


def frequencies(head_size):
    half_size = head_size // 2
    return jnp.exp(jnp.arange(half_size, dtype=jnp.float32) * (-2.0 * math.log(THETA) / head_size))


def rotate(value, cosine, sine_part):
    half_size = value.shape[-1] // 2
    leading = value[..., :half_size]
    trailing = value[..., half_size:]
    return jnp.concatenate(
        [leading * cosine - trailing * sine_part, trailing * cosine + leading * sine_part], axis=-1
    )


def doc_info(starts, positions):
    below = starts[None, :] <= positions[:, None]
    doc_ids = jnp.sum(below.astype(jnp.int32), axis=1)
    begins = jnp.max(jnp.where(below, starts[None, :], 0), axis=1)
    return (doc_ids, positions - begins)


def norm_forward(value, gain_vec):
    inverse = lax.rsqrt(jnp.mean(value * value, axis=-1, keepdims=True) + EPSILON)
    return (value * inverse * gain_vec, inverse)


def norm_backward(value, inverse, gain_vec, grad_in):
    scaled = grad_in * gain_vec
    inner_mean = jnp.mean(scaled * value, axis=-1, keepdims=True)
    grad_value = inverse * (scaled - value * inverse * inverse * inner_mean)
    grad_gain = jnp.sum((grad_in * value * inverse).reshape(-1, value.shape[-1]), axis=0)
    return (grad_value, grad_gain)


def product(left, right, form):
    return jnp.einsum(form, left, right, preferred_element_type=jnp.float32)


class Links:
    def __init__(self, n_dp, n_ctx):
        self.n_dp = n_dp
        self.n_ctx = n_ctx
        self.n_chip = n_ctx // 2
        self.dp = lax.axis_index("dp")
        ctx = lax.axis_index("ctx")
        self.core = lax.rem(ctx, 2)
        self.chip = ctx // 2
        self.first = self.core == 0

    def send(self, value, target):
        pairs = []
        for d in range(self.n_dp):
            for c in range(self.n_ctx):
                to_d, to_c = target(d, c)
                if 0 <= to_c < self.n_ctx:
                    pairs.append((d * self.n_ctx + c, to_d * self.n_ctx + to_c))
        return lax.ppermute(value, ("dp", "ctx"), pairs)

    def to_core(self, value):
        return self.send(value, lambda d, c: (d, c ^ 1))

    def to_near(self, value):
        return self.send(value, lambda d, c: (d ^ (1 + c % 2), c))

    def to_far(self, value):
        return self.send(value, lambda d, c: (d ^ (2 - c % 2), c))

    def to_chip(self, value, bit):
        return self.send(value, lambda d, c: (d, c ^ (2 << bit)))

    def up(self, value):
        return self.send(value, lambda d, c: (d, c + 2))

    def down(self, value):
        return self.send(value, lambda d, c: (d, c - 2))

    def swap(self, flag, left, right):
        return (jnp.where(flag, right, left), jnp.where(flag, left, right))

    def in_order(self, mine, other, axis):
        left, right = self.swap(self.core == 1, mine, other)
        return jnp.concatenate([left, right], axis=axis)

    def flip(self, blocks):
        odd, high = (self.dp & 1) == 1, (self.dp & 2) == 2
        b0, b1, b2, b3 = blocks
        b0, b1 = self.swap(odd, b0, b1)
        b2, b3 = self.swap(odd, b2, b3)
        b0, b2 = self.swap(high, b0, b2)
        b1, b3 = self.swap(high, b1, b3)
        return [b0, b1, b2, b3]

    def absolute(self, blocks):
        own, near, far, both = blocks
        near, far = self.swap(self.core == 1, near, far)
        return self.flip([own, near, far, both])

    def relative(self, blocks):
        own, near, far, both = self.flip(blocks)
        near, far = self.swap(self.core == 1, near, far)
        return [own, near, far, both]

    def gather(self, own):
        near = self.to_near(own)
        far = self.to_far(own)
        both = self.to_far(near)
        mine = [own, near, far, both]
        other = [self.to_core(item) for item in (own, far, near, both)]
        return (mine, other)

    def reduce(self, mine, other):
        low = jnp.bfloat16
        f32 = jnp.float32
        out = jnp.concatenate([other[i].astype(low) for i in (0, 2, 1, 3)], axis=0)
        got = self.to_core(out)
        size = mine[0].shape[0]
        own, near, far, both = [
            mine[i] + got[i * size : (i + 1) * size].astype(f32) for i in range(4)
        ]
        got = self.to_far(jnp.concatenate([far.astype(low), both.astype(low)], axis=0))
        near = near + got[size:].astype(f32)
        got_near = self.to_near(near.astype(low))
        total = own + got[:size].astype(f32) + got_near.astype(f32)
        bits = self.n_chip.bit_length() - 1
        for bit in range(bits):
            flag = ((self.chip >> bit) & 1) == 1
            size = total.shape[0] // 2
            keep, give = self.swap(flag, total[:size], total[size:])
            total = keep + self.to_chip(give.astype(low), bit).astype(f32)
        total = total.astype(low)
        for bit in reversed(range(bits)):
            flag = ((self.chip >> bit) & 1) == 1
            left, right = self.swap(flag, total, self.to_chip(total, bit))
            total = jnp.concatenate([left, right], axis=0)
        return (total, self.to_core(total))


def key_allowed(links, row_count, at, block, q_pos, q_doc, starts):
    place = at + jnp.arange(block, dtype=jnp.int32)
    step = place // (2 * row_count)
    within = lax.rem(place, 2 * row_count)
    side = within // row_count
    core = jnp.where(side == 0, links.core, 1 - links.core)
    key_pos = ((links.chip - step) * 2 + core) * row_count + lax.rem(within, row_count)
    key_doc, unused_offsets = doc_info(starts, key_pos)
    return (
        (key_pos[None, :] >= 0)
        & (key_pos[None, :] <= q_pos[:, None])
        & (key_doc[None, :] == q_doc[:, None])
    )


def key_blocks(count):
    block = math.gcd(count, 1024)
    return (block, count // block)


def fold_keys(links, row_count, key_rows, value_rows, query, q_pos, q_doc, starts):
    block, steps = key_blocks(key_rows.shape[0])
    rows = query.shape[0]
    width = query.shape[1]
    factor = 1.0 / math.sqrt(width)

    def fold_step(state_old, block_index):
        at = block_index * block
        key_block = lax.dynamic_slice_in_dim(key_rows, at, block, 0)
        value_block = lax.dynamic_slice_in_dim(value_rows, at, block, 0)
        peak_old, denominator, accumulated = state_old
        allowed = key_allowed(links, row_count, at, block, q_pos, q_doc, starts)
        scores = product(query, key_block, "re,ke->rk") * factor
        scores = jnp.where(allowed, scores, NEGATIVE)
        peak_new = jnp.maximum(peak_old, jnp.max(scores, axis=-1))
        weights = jnp.where(allowed, jnp.exp(scores - peak_new[:, None]), 0.0)
        shrink = jnp.exp(peak_old - peak_new)
        denominator = denominator * shrink + jnp.sum(weights, axis=-1)
        accumulated = accumulated * shrink[:, None] + product(
            weights.astype(jnp.bfloat16), value_block, "rk,ke->re"
        )
        return ((peak_new, denominator, accumulated), None)

    initial = (
        jnp.full((rows,), NEGATIVE, jnp.float32),
        jnp.zeros((rows,), jnp.float32),
        jnp.zeros((rows, width), jnp.float32),
    )
    state_out, unused_stack = lax.scan(
        fold_step, initial, jnp.arange(steps, dtype=jnp.int32), unroll=math.gcd(steps, 2)
    )
    return state_out


def back_keys(
    links, row_count, key_rows, value_rows, query, d_heads, log_total, delta, q_pos, q_doc, starts
):
    block, steps = key_blocks(key_rows.shape[0])
    width = query.shape[1]
    factor = 1.0 / math.sqrt(width)

    def back_step(d_old, block_index):
        at = block_index * block
        key_block = lax.dynamic_slice_in_dim(key_rows, at, block, 0)
        value_block = lax.dynamic_slice_in_dim(value_rows, at, block, 0)
        allowed = key_allowed(links, row_count, at, block, q_pos, q_doc, starts)
        scores = product(query, key_block, "re,ke->rk") * factor
        scores = jnp.where(allowed, scores, NEGATIVE)
        probs = jnp.where(allowed, jnp.exp(scores - log_total[:, None]), 0.0)
        d_probs = product(d_heads, value_block, "re,ke->rk")
        d_scores = (probs * (d_probs - delta[:, None])).astype(jnp.bfloat16)
        d_new = d_old + product(d_scores, key_block, "rk,ke->re") * factor
        d_values = product(probs.astype(jnp.bfloat16), d_heads, "rk,re->ke")
        d_keys = product(d_scores, query, "rk,re->ke") * factor
        return (d_new, jnp.concatenate([d_keys, d_values], axis=1))

    d_query, stacked = lax.scan(
        back_step,
        jnp.zeros(query.shape, jnp.float32),
        jnp.arange(steps, dtype=jnp.int32),
        unroll=math.gcd(steps, 2),
    )
    return (d_query, stacked.reshape(block * steps, 2 * width))


GAIN_ROWS = 32


def local(
    tokens,
    doc_starts,
    attn_gain,
    query_gain,
    key_gain,
    post_attn_gain,
    ffw_gain,
    post_ffw_gain,
    w_query,
    w_key,
    w_value,
    w_out,
    w_gate,
    w_up,
    w_down,
    cotangent,
    n_dp,
    n_ctx,
):
    links = Links(n_dp, n_ctx)
    f32 = jnp.float32
    low = jnp.bfloat16
    width = tokens.shape[2]
    gains = (attn_gain, query_gain, key_gain, post_attn_gain, ffw_gain, post_ffw_gain)
    gain_sizes = [item.shape[0] for item in gains]
    cols_k = w_key.shape[1]
    head_size = w_query.shape[1]
    side = head_size // 2
    half = width // 2
    span = w_gate.shape[1] // 2
    at_kv = 2 * width
    at_gain = at_kv + half
    gain_used = sum(gain_sizes) // side

    def core_part(value, axis):
        size = value.shape[axis] // 2
        first = lax.slice_in_dim(value, 0, size, axis=axis)
        second = lax.slice_in_dim(value, size, 2 * size, axis=axis)
        return jnp.where(links.first, first, second)

    gain_block = jnp.concatenate(gains).reshape(gain_used, side)
    gain_block = jnp.pad(gain_block, ((0, GAIN_ROWS - gain_used), (0, 0)))
    attn_own = jnp.concatenate(
        [
            core_part(w_query, 1),
            jnp.transpose(core_part(w_out, 0)),
            core_part(jnp.concatenate([w_key, w_value], axis=1), 0),
            gain_block,
        ],
        axis=0,
    )
    ffw_own = jnp.concatenate(
        [core_part(w_gate, 1), core_part(w_up, 1), jnp.transpose(core_part(w_down, 0))], axis=0
    )
    attn_mine, attn_other = links.gather(attn_own)
    ffw_mine, ffw_other = links.gather(ffw_own)

    gain_all = jnp.stack(
        links.absolute([item[at_gain : at_gain + gain_used] for item in attn_mine])
    ).reshape(n_dp, gain_used * side)
    gain_list = []
    at = 0
    for size in gain_sizes:
        gain_list.append(gain_all[:, at : at + size].reshape(-1).astype(f32))
        at += size
    g_attn, g_query, g_key, g_post, g_ffw, g_pffw = gain_list

    def head_columns(start):
        parts = []
        for mine, other in zip(attn_mine, attn_other):
            parts.extend(
                links.swap(
                    links.core == 1, mine[start : start + width], other[start : start + width]
                )
            )
        return jnp.concatenate(parts, axis=1)

    wq_full = head_columns(0)
    wo_turned = head_columns(width)
    wkv_full = jnp.concatenate(
        [
            links.in_order(mine[at_kv:at_gain], other[at_kv:at_gain], 0)
            for mine, other in zip(attn_mine, attn_other)
        ],
        axis=1,
    )
    ffw_pieces = []
    for mine, other in zip(ffw_mine, ffw_other):
        ffw_pieces.extend((mine, other))

    def ffw_columns(index):
        return jnp.concatenate(
            [item[index * width : (index + 1) * width] for item in ffw_pieces], axis=1
        )

    wg_full, wu_full, wd_turned = [ffw_columns(index) for index in range(3)]

    row_count = tokens.shape[1]
    starts = doc_starts[0]
    positions = lax.axis_index("ctx") * row_count + jnp.arange(row_count, dtype=jnp.int32)
    doc_ids, offsets = doc_info(starts, positions)
    angles = offsets.astype(jnp.float32)[:, None] * frequencies(head_size)[None, :]
    cosine = jnp.cos(angles)
    sine_part = jnp.sin(angles)
    stream = tokens[0].astype(jnp.float32)
    normed, attn_inverse = norm_forward(stream, g_attn)
    normed_low = normed.astype(low)

    def to_heads(value):
        return jnp.stack([value[:, h * head_size : (h + 1) * head_size] for h in range(n_dp)])

    def from_heads(value):
        return jnp.concatenate([value[h] for h in range(n_dp)], axis=1)

    key_value_raw = product(normed_low, wkv_full, "td,da->ta")
    wide = 2 * cols_k
    kv_blocks = links.absolute([key_value_raw[:, i * wide : (i + 1) * wide] for i in range(n_dp)])
    key_raw = jnp.concatenate([item[:, :cols_k] for item in kv_blocks], axis=1)
    value_low = jnp.concatenate([item[:, cols_k:] for item in kv_blocks], axis=1).astype(low)
    key_normed, key_inverse = norm_forward(key_raw, g_key)
    key_low = rotate(key_normed, cosine, sine_part).astype(low)
    moving = jnp.concatenate([key_low, value_low], axis=1)
    pieces = []
    for step in range(links.n_chip):
        pieces.extend((moving, links.to_core(moving)))
        if step + 1 < links.n_chip:
            moving = links.up(moving)
    key_value = jnp.concatenate(pieces, axis=0)
    key_whole = key_value[:, :head_size]
    value_whole = key_value[:, head_size:]

    query_raw = to_heads(product(normed_low, wq_full, "td,da->ta"))
    query_normed, query_inverse = norm_forward(query_raw, g_query)
    query_low = rotate(query_normed, cosine[None], sine_part[None]).astype(low)
    query_low = query_low.reshape(n_dp * row_count, head_size)
    q_pos = jnp.tile(positions, n_dp)
    q_doc = jnp.tile(doc_ids, n_dp)
    peak, denominator, accumulated = fold_keys(
        links, row_count, key_whole, value_whole, query_low, q_pos, q_doc, starts
    )
    log_total = peak + jnp.log(denominator)
    attended = accumulated / denominator[:, None]
    attended_low = from_heads(attended.astype(low).reshape(n_dp, row_count, head_size))
    branch = product(attended_low, wo_turned, "ta,da->td")
    post_branch, post_inverse = norm_forward(branch, g_post)
    hidden_state = stream + post_branch
    ffw_normed, ffw_inverse = norm_forward(hidden_state, g_ffw)
    ffw_low = ffw_normed.astype(low)
    gate_act = product(ffw_low, wg_full, "td,df->tf")
    up_act = product(ffw_low, wu_full, "td,df->tf")
    inner_act, inner_back = jax.vjp(
        lambda left, right: jax.nn.gelu(left, approximate=True) * right, gate_act, up_act
    )
    inner_low = inner_act.astype(low)
    down_out = product(inner_low, wd_turned, "tf,df->td")
    ffw_branch, down_inverse = norm_forward(down_out, g_pffw)
    output = (hidden_state + ffw_branch).astype(low)
    grad_output = cotangent[0].astype(f32)
    d_down, dg_pffw = norm_backward(down_out, down_inverse, g_pffw, grad_output)
    d_down_low = d_down.astype(low)
    dw_down = product(d_down_low, inner_low, "td,tf->df")
    d_inner = product(d_down_low, wd_turned, "td,df->tf")
    d_gate, d_up = inner_back(d_inner)
    d_gate_low = d_gate.astype(low)
    d_up_low = d_up.astype(low)
    dw_gate = product(ffw_low, d_gate_low, "td,tf->df")
    dw_up = product(ffw_low, d_up_low, "td,tf->df")

    def ffw_grad(index):
        return jnp.concatenate(
            [item[:, index * span : (index + 1) * span] for item in (dw_gate, dw_up, dw_down)],
            axis=0,
        )

    ffw_totals = links.reduce(
        [ffw_grad(2 * i) for i in range(n_dp)], [ffw_grad(2 * i + 1) for i in range(n_dp)]
    )
    d_ffw_in = product(d_gate_low, wg_full, "tf,df->td") + product(d_up_low, wu_full, "tf,df->td")
    d_hidden_part, dg_ffw = norm_backward(hidden_state, ffw_inverse, g_ffw, d_ffw_in)
    d_hidden = grad_output + d_hidden_part
    d_branch, dg_post = norm_backward(branch, post_inverse, g_post, d_hidden)
    d_branch_low = d_branch.astype(low)
    dw_out = product(d_branch_low, attended_low, "td,ta->da")
    d_attended = to_heads(product(d_branch_low, wo_turned, "td,da->ta").astype(low))
    d_heads = d_attended.reshape(n_dp * row_count, head_size)
    delta = jnp.sum(d_heads.astype(f32) * attended, axis=-1)
    d_query, d_key_value = back_keys(
        links,
        row_count,
        key_whole,
        value_whole,
        query_low,
        d_heads,
        log_total,
        delta,
        q_pos,
        q_doc,
        starts,
    )
    d_key_value = d_key_value.reshape(links.n_chip, 2, row_count, 2 * head_size)
    d_key_value = d_key_value[:, 0] + links.to_core(d_key_value[:, 1].astype(low)).astype(f32)
    d_moving = d_key_value[links.n_chip - 1]
    for step in range(1, links.n_chip):
        d_moving = d_key_value[links.n_chip - 1 - step] + links.down(d_moving.astype(low)).astype(
            f32
        )
    d_value_low = d_moving[:, head_size:].astype(low)
    d_key_normed = rotate(d_moving[:, :head_size], cosine, -sine_part)
    d_key_raw, dg_key = norm_backward(key_raw, key_inverse, g_key, d_key_normed)
    d_key_low = d_key_raw.astype(low)
    d_query_normed = rotate(
        d_query.reshape(n_dp, row_count, head_size), cosine[None], -sine_part[None]
    )
    d_query_raw, dg_query = norm_backward(query_raw, query_inverse, g_query, d_query_normed)
    d_query_low = from_heads(d_query_raw.astype(low))
    d_kv_low = jnp.concatenate(
        links.relative(
            [
                jnp.concatenate(
                    [
                        d_key_low[:, i * cols_k : (i + 1) * cols_k],
                        d_value_low[:, i * cols_k : (i + 1) * cols_k],
                    ],
                    axis=1,
                )
                for i in range(n_dp)
            ]
        ),
        axis=1,
    )
    dw_query = product(normed_low, d_query_low, "td,ta->da")
    dw_kv = product(normed_low, d_kv_low, "td,ta->da")
    d_normed = product(d_query_low, wq_full, "ta,da->td") + product(d_kv_low, wkv_full, "ta,da->td")
    d_stream_part, dg_attn = norm_backward(stream, attn_inverse, g_attn, d_normed)
    grad_tokens = (d_hidden + d_stream_part).astype(low)

    gain_grads = jnp.concatenate(
        [item.reshape(n_dp, -1) for item in (dg_attn, dg_query, dg_key, dg_post, dg_ffw, dg_pffw)],
        axis=1,
    ).reshape(n_dp, gain_used, side)
    gain_grads = jnp.pad(gain_grads, ((0, 0), (0, GAIN_ROWS - gain_used), (0, 0)))
    gain_blocks = links.relative([gain_grads[i] for i in range(n_dp)])
    attn_mine, attn_other = [], []
    for i in range(n_dp):
        left = i * head_size
        middle = left + side
        right = left + head_size
        kv_part = dw_kv[:, i * wide : (i + 1) * wide]
        mine, other = links.swap(
            links.core == 1,
            jnp.concatenate([dw_query[:, left:middle], dw_out[:, left:middle], kv_part[:half]]),
            jnp.concatenate([dw_query[:, middle:right], dw_out[:, middle:right], kv_part[half:]]),
        )
        attn_mine.append(jnp.concatenate([mine, gain_blocks[i]], axis=0))
        attn_other.append(jnp.concatenate([other, gain_blocks[i]], axis=0))
    attn_total, attn_rest = links.reduce(attn_mine, attn_other)
    ffw_total = links.in_order(ffw_totals[0], ffw_totals[1], 1).astype(f32)
    t_heads = links.in_order(attn_total[:at_kv], attn_rest[:at_kv], 1).astype(f32)
    t_kv = links.in_order(attn_total[at_kv:at_gain], attn_rest[at_kv:at_gain], 0).astype(f32)
    t_gain = attn_total[at_gain : at_gain + gain_used].reshape(-1).astype(f32)
    gain_out = []
    at = 0
    for size in gain_sizes:
        gain_out.append(t_gain[at : at + size])
        at += size
    return (
        (output[None], grad_tokens[None])
        + tuple(gain_out)
        + (
            t_heads[:width],
            t_kv[:, :cols_k],
            t_kv[:, cols_k:],
            jnp.transpose(t_heads[width:]),
            ffw_total[:width],
            ffw_total[width : 2 * width],
            jnp.transpose(ffw_total[2 * width :]),
        )
    )


def solution(mesh):
    placed = (
        P("dp", "ctx", None),
        P("dp", None),
        P("dp"),
        P("dp"),
        P("dp"),
        P("dp"),
        P("dp"),
        P("dp"),
        P(None, "dp"),
        P(None, "dp"),
        P(None, "dp"),
        P("dp", None),
        P(None, "dp"),
        P(None, "dp"),
        P("dp", None),
        P("dp", "ctx", None),
    )
    return jax.shard_map(
        functools.partial(local, n_dp=mesh.shape["dp"], n_ctx=mesh.shape["ctx"]),
        mesh=mesh,
        in_specs=placed,
        out_specs=(
            P("dp", "ctx", None),
            P("dp", "ctx", None),
            P("dp"),
            P("dp"),
            P("dp"),
            P("dp"),
            P("dp"),
            P("dp"),
            P(None, "dp"),
            P(None, "dp"),
            P(None, "dp"),
            P("dp", None),
            P(None, "dp"),
            P(None, "dp"),
            P("dp", None),
        ),
        check_vma=False,
    )
```

```python
import functools
import math

import jax
import jax.numpy as jnp
from jax import lax
from jax.sharding import PartitionSpec as P

EPSILON = 1e-06
THETA = 1000000.0
NEGATIVE = -1e30


def frequencies(head_size):
    half_size = head_size // 2
    return jnp.exp(jnp.arange(half_size, dtype=jnp.float32) * (-2.0 * math.log(THETA) / head_size))


def rotate(value, cosine, sine_part):
    half_size = value.shape[-1] // 2
    leading = value[..., :half_size]
    trailing = value[..., half_size:]
    return jnp.concatenate(
        [leading * cosine - trailing * sine_part, trailing * cosine + leading * sine_part], axis=-1
    )


def doc_info(starts, positions):
    below = starts[None, :] <= positions[:, None]
    doc_ids = jnp.sum(below.astype(jnp.int32), axis=1)
    begins = jnp.max(jnp.where(below, starts[None, :], 0), axis=1)
    return (doc_ids, positions - begins)


def norm_forward(value, gain_vec):
    inverse = lax.rsqrt(jnp.mean(value * value, axis=-1, keepdims=True) + EPSILON)
    return (value * inverse * gain_vec, inverse)


def norm_backward(value, inverse, gain_vec, grad_in):
    scaled = grad_in * gain_vec
    inner_mean = jnp.mean(scaled * value, axis=-1, keepdims=True)
    grad_value = inverse * (scaled - value * inverse * inverse * inner_mean)
    grad_gain = jnp.sum((grad_in * value * inverse).reshape(-1, value.shape[-1]), axis=0)
    return (grad_value, grad_gain)


def product(left, right, form):
    return jnp.einsum(form, left, right, preferred_element_type=jnp.float32)


class Links:
    def __init__(self, n_dp, n_ctx):
        self.n_dp = n_dp
        self.n_ctx = n_ctx
        self.n_chip = n_ctx // 2
        self.dp = lax.axis_index("dp")
        ctx = lax.axis_index("ctx")
        self.core = lax.rem(ctx, 2)
        self.chip = ctx // 2
        self.first = self.core == 0

    def send(self, value, target):
        pairs = []
        for d in range(self.n_dp):
            for c in range(self.n_ctx):
                to_d, to_c = target(d, c)
                if 0 <= to_c < self.n_ctx:
                    pairs.append((d * self.n_ctx + c, to_d * self.n_ctx + to_c))
        return lax.ppermute(value, ("dp", "ctx"), pairs)

    def to_core(self, value):
        return self.send(value, lambda d, c: (d, c ^ 1))

    def to_near(self, value):
        return self.send(value, lambda d, c: (d ^ (1 + c % 2), c))

    def to_far(self, value):
        return self.send(value, lambda d, c: (d ^ (2 - c % 2), c))

    def to_chip(self, value, mask):
        return self.send(value, lambda d, c: (d, c ^ (2 * mask)))

    def up(self, value):
        return self.send(value, lambda d, c: (d, c + 2))

    def down(self, value):
        return self.send(value, lambda d, c: (d, c - 2))

    def swap(self, flag, left, right):
        return (jnp.where(flag, right, left), jnp.where(flag, left, right))

    def in_order(self, mine, other, axis):
        left, right = self.swap(self.core == 1, mine, other)
        return jnp.concatenate([left, right], axis=axis)

    def flip(self, blocks):
        odd, high = (self.dp & 1) == 1, (self.dp & 2) == 2
        b0, b1, b2, b3 = blocks
        b0, b1 = self.swap(odd, b0, b1)
        b2, b3 = self.swap(odd, b2, b3)
        b0, b2 = self.swap(high, b0, b2)
        b1, b3 = self.swap(high, b1, b3)
        return [b0, b1, b2, b3]

    def absolute(self, blocks):
        own, near, far, both = blocks
        near, far = self.swap(self.core == 1, near, far)
        return self.flip([own, near, far, both])

    def relative(self, blocks):
        own, near, far, both = self.flip(blocks)
        near, far = self.swap(self.core == 1, near, far)
        return [own, near, far, both]

    def gather(self, own):
        near = self.to_near(own)
        far = self.to_far(own)
        both = self.to_far(near)
        mine = [own, near, far, both]
        other = [self.to_core(item) for item in (own, far, near, both)]
        return (mine, other)

    def core_rest(self, other):
        return jnp.concatenate([other[i].astype(jnp.bfloat16) for i in (0, 2, 1, 3)], axis=0)

    def core_sum(self, mine, got):
        size = mine[0].shape[0]
        return [
            mine[i] + got[i * size : (i + 1) * size].astype(jnp.float32) for i in range(4)
        ]

    def far_rest(self, sums):
        return jnp.concatenate([item.astype(jnp.bfloat16) for item in sums[2:]], axis=0)

    def far_sum(self, sums, got):
        size = sums[0].shape[0]
        return (
            sums[0] + got[:size].astype(jnp.float32),
            sums[1] + got[size:].astype(jnp.float32),
        )

    def digits(self):
        bits = self.n_chip.bit_length() - 1
        return [(bit, min(2, bits - bit)) for bit in range(0, bits, 2)]

    def chip_scatter(self, total):
        for bit, count in self.digits():
            radix = 1 << count
            digit = (self.chip >> bit) & (radix - 1)
            size = total.shape[0] // radix
            value = lax.dynamic_slice_in_dim(total, digit * size, size, 0)
            for mask in range(1, radix):
                part = lax.dynamic_slice_in_dim(total, (digit ^ mask) * size, size, 0)
                part = self.to_chip(part.astype(jnp.bfloat16), mask << bit)
                value = value + part.astype(jnp.float32)
            total = value
        return total.astype(jnp.bfloat16)

    def chip_gather(self, total):
        for bit, count in reversed(self.digits()):
            radix = 1 << count
            parts = [total] + [self.to_chip(total, mask << bit) for mask in range(1, radix)]
            for place in range(count):
                flag = ((self.chip >> (bit + place)) & 1) == 1
                for i in range(radix):
                    if not i & (1 << place):
                        j = i | (1 << place)
                        parts[i], parts[j] = self.swap(flag, parts[i], parts[j])
            total = jnp.concatenate(parts, axis=0)
        return (total, self.to_core(total))


def tie(*values):
    return lax.optimization_barrier(values)


def key_allowed(links, row_count, at, block, q_pos, q_doc, starts):
    place = at + jnp.arange(block, dtype=jnp.int32)
    step = place // (2 * row_count)
    within = lax.rem(place, 2 * row_count)
    side = within // row_count
    core = jnp.where(side == 0, links.core, 1 - links.core)
    key_pos = ((links.chip - step) * 2 + core) * row_count + lax.rem(within, row_count)
    key_doc, unused_offsets = doc_info(starts, key_pos)
    return (
        (key_pos[None, :] >= 0)
        & (key_pos[None, :] <= q_pos[:, None])
        & (key_doc[None, :] == q_doc[:, None])
    )


def fold_keys(links, row_count, pieces, query, q_pos, q_doc, starts):
    rows, width = query.shape
    factor = 1.0 / math.sqrt(width)
    peak = jnp.full((rows,), NEGATIVE, jnp.float32)
    denominator = jnp.zeros((rows,), jnp.float32)
    accumulated = jnp.zeros((rows, width), jnp.float32)
    at = 0
    for piece in pieces:
        block = piece.shape[0]
        allowed = key_allowed(links, row_count, at, block, q_pos, q_doc, starts)
        at += block
        scores = product(query, piece[:, :width], "re,ke->rk") * factor
        scores = jnp.where(allowed, scores, NEGATIVE)
        peak_new = jnp.maximum(peak, jnp.max(scores, axis=-1))
        weights = jnp.where(allowed, jnp.exp(scores - peak_new[:, None]), 0.0)
        shrink = jnp.exp(peak - peak_new)
        denominator = denominator * shrink + jnp.sum(weights, axis=-1)
        accumulated = accumulated * shrink[:, None] + product(
            weights.astype(jnp.bfloat16), piece[:, width:], "rk,ke->re"
        )
        peak = peak_new
    return (peak, denominator, accumulated)


def back_keys(
    links, row_count, pieces, query, d_heads, log_total, delta, q_pos, q_doc, starts
):
    width = query.shape[1]
    factor = 1.0 / math.sqrt(width)
    d_query = jnp.zeros(query.shape, jnp.float32)
    d_mine, d_other = [], []
    at = sum(piece.shape[0] for piece in pieces)
    for piece in reversed(pieces):
        block = piece.shape[0]
        at -= block
        key_block, value_block = piece[:, :width], piece[:, width:]
        allowed = key_allowed(links, row_count, at, block, q_pos, q_doc, starts)
        scores = product(query, key_block, "re,ke->rk") * factor
        scores = jnp.where(allowed, scores, NEGATIVE)
        probs = jnp.where(allowed, jnp.exp(scores - log_total[:, None]), 0.0)
        d_probs = product(d_heads, value_block, "re,ke->rk")
        d_scores = (probs * (d_probs - delta[:, None])).astype(jnp.bfloat16)
        d_query = d_query + product(d_scores, key_block, "rk,ke->re") * factor
        d_values = product(probs.astype(jnp.bfloat16), d_heads, "rk,re->ke")
        d_keys = product(d_scores, query, "rk,re->ke") * factor
        joined = jnp.concatenate([d_keys, d_values], axis=1)
        joined = joined.reshape(block // (2 * row_count), 2, row_count, 2 * width)
        arrived = links.to_core(joined[:, 1].astype(jnp.bfloat16))
        for step in reversed(range(joined.shape[0])):
            d_mine.append(joined[step, 0])
            d_other.append(arrived[step])
    return (d_query, d_mine, d_other)


GAIN_ROWS = 64


def local(
    tokens,
    doc_starts,
    attn_gain,
    query_gain,
    key_gain,
    post_attn_gain,
    ffw_gain,
    post_ffw_gain,
    w_query,
    w_key,
    w_value,
    w_out,
    w_gate,
    w_up,
    w_down,
    cotangent,
    n_dp,
    n_ctx,
):
    links = Links(n_dp, n_ctx)
    f32 = jnp.float32
    low = jnp.bfloat16
    width = tokens.shape[2]
    gains = (attn_gain, query_gain, key_gain, post_attn_gain, ffw_gain, post_ffw_gain)
    gain_sizes = [item.shape[0] for item in gains]
    cols_k = w_key.shape[1]
    head_size = w_query.shape[1]
    side = head_size // 2
    half = width // 2
    span = w_gate.shape[1] // 2
    at_kv = 2 * width
    at_gain = at_kv + half
    gain_used = sum(gain_sizes) // side

    def core_part(value, axis):
        size = value.shape[axis] // 2
        first = lax.slice_in_dim(value, 0, size, axis=axis)
        second = lax.slice_in_dim(value, size, 2 * size, axis=axis)
        return jnp.where(links.first, first, second)

    gain_block = jnp.concatenate(gains).reshape(gain_used, side)
    gain_block = jnp.pad(gain_block, ((0, GAIN_ROWS - gain_used), (0, 0)))
    attn_own = jnp.concatenate(
        [
            core_part(w_query, 1),
            jnp.transpose(core_part(w_out, 0)),
            core_part(jnp.concatenate([w_key, w_value], axis=1), 0),
            gain_block,
        ],
        axis=0,
    )
    ffw_own = jnp.concatenate(
        [core_part(w_gate, 1), core_part(w_up, 1), jnp.transpose(core_part(w_down, 0))], axis=0
    )
    attn_mine, attn_other = links.gather(attn_own)
    ffw_own, attn_last = tie(ffw_own, attn_mine[3])
    attn_mine[3] = attn_last
    ffw_mine, ffw_other = links.gather(ffw_own)

    gain_all = jnp.stack(
        links.absolute([item[at_gain : at_gain + gain_used] for item in attn_mine])
    ).reshape(n_dp, gain_used * side)
    gain_list = []
    at = 0
    for size in gain_sizes:
        gain_list.append(gain_all[:, at : at + size].reshape(-1).astype(f32))
        at += size
    g_attn, g_query, g_key, g_post, g_ffw, g_pffw = gain_list

    def head_columns(start):
        parts = []
        for mine, other in zip(attn_mine, attn_other):
            parts.extend(
                links.swap(
                    links.core == 1, mine[start : start + width], other[start : start + width]
                )
            )
        return jnp.concatenate(parts, axis=1)

    wq_full = head_columns(0)
    wo_turned = head_columns(width)
    wkv_full = jnp.concatenate(
        [
            links.in_order(mine[at_kv:at_gain], other[at_kv:at_gain], 0)
            for mine, other in zip(attn_mine, attn_other)
        ],
        axis=1,
    )
    ffw_pieces = []
    for mine, other in zip(ffw_mine, ffw_other):
        ffw_pieces.extend((mine, other))

    def ffw_columns(index):
        return jnp.concatenate(
            [item[index * width : (index + 1) * width] for item in ffw_pieces], axis=1
        )

    wg_full, wu_full, wd_turned = [ffw_columns(index) for index in range(3)]

    row_count = tokens.shape[1]
    starts = doc_starts[0]
    positions = lax.axis_index("ctx") * row_count + jnp.arange(row_count, dtype=jnp.int32)
    doc_ids, offsets = doc_info(starts, positions)
    angles = offsets.astype(jnp.float32)[:, None] * frequencies(head_size)[None, :]
    cosine = jnp.cos(angles)
    sine_part = jnp.sin(angles)
    stream = tokens[0].astype(jnp.float32)
    normed, attn_inverse = norm_forward(stream, g_attn)
    normed_low = normed.astype(low)

    def to_heads(value):
        return jnp.stack([value[:, h * head_size : (h + 1) * head_size] for h in range(n_dp)])

    def from_heads(value):
        return jnp.concatenate([value[h] for h in range(n_dp)], axis=1)

    key_value_raw = product(normed_low, wkv_full, "td,da->ta")
    wide = 2 * cols_k
    kv_blocks = links.absolute([key_value_raw[:, i * wide : (i + 1) * wide] for i in range(n_dp)])
    key_raw = jnp.concatenate([item[:, :cols_k] for item in kv_blocks], axis=1)
    value_low = jnp.concatenate([item[:, cols_k:] for item in kv_blocks], axis=1).astype(low)
    key_normed, key_inverse = norm_forward(key_raw, g_key)
    key_low = rotate(key_normed, cosine, sine_part).astype(low)
    moving = jnp.concatenate([key_low, value_low], axis=1)
    pieces = []
    for step in range(links.n_chip):
        pieces.extend((moving, links.to_core(moving)))
        if step + 1 < links.n_chip:
            moving = links.up(moving)
    group = 2 * math.gcd(links.n_chip, 2)
    pieces = [
        jnp.concatenate(pieces[i : i + group], axis=0) for i in range(0, len(pieces), group)
    ]

    query_raw = to_heads(product(normed_low, wq_full, "td,da->ta"))
    query_normed, query_inverse = norm_forward(query_raw, g_query)
    query_low = rotate(query_normed, cosine[None], sine_part[None]).astype(low)
    query_low = query_low.reshape(n_dp * row_count, head_size)
    q_pos = jnp.tile(positions, n_dp)
    q_doc = jnp.tile(doc_ids, n_dp)
    peak, denominator, accumulated = fold_keys(
        links, row_count, pieces, query_low, q_pos, q_doc, starts
    )
    log_total = peak + jnp.log(denominator)
    attended = accumulated / denominator[:, None]
    attended_low = from_heads(attended.astype(low).reshape(n_dp, row_count, head_size))
    branch = product(attended_low, wo_turned, "ta,da->td")
    post_branch, post_inverse = norm_forward(branch, g_post)
    hidden_state = stream + post_branch
    ffw_normed, ffw_inverse = norm_forward(hidden_state, g_ffw)
    ffw_low = ffw_normed.astype(low)
    gate_act = product(ffw_low, wg_full, "td,df->tf")
    up_act = product(ffw_low, wu_full, "td,df->tf")
    inner_act, inner_back = jax.vjp(
        lambda left, right: jax.nn.gelu(left, approximate=True) * right, gate_act, up_act
    )
    inner_low = inner_act.astype(low)
    down_out = product(inner_low, wd_turned, "tf,df->td")
    ffw_branch, down_inverse = norm_forward(down_out, g_pffw)
    output = (hidden_state + ffw_branch).astype(low)
    grad_output = cotangent[0].astype(f32)
    d_down, dg_pffw = norm_backward(down_out, down_inverse, g_pffw, grad_output)
    d_down_low = d_down.astype(low)
    dw_down = product(d_down_low, inner_low, "td,tf->df")
    d_inner = product(d_down_low, wd_turned, "td,df->tf")
    d_gate, d_up = inner_back(d_inner)
    d_gate_low = d_gate.astype(low)
    d_up_low = d_up.astype(low)
    dw_gate = product(ffw_low, d_gate_low, "td,tf->df")
    dw_up = product(ffw_low, d_up_low, "td,tf->df")

    def ffw_grad(index):
        return jnp.concatenate(
            [item[:, index * span : (index + 1) * span] for item in (dw_gate, dw_up, dw_down)],
            axis=0,
        )

    ffw_part = [ffw_grad(2 * i) for i in range(n_dp)]
    ffw_out = links.core_rest([ffw_grad(2 * i + 1) for i in range(n_dp)])
    d_gate_low, d_up_low, ffw_out = tie(d_gate_low, d_up_low, ffw_out)
    ffw_got = links.to_core(ffw_out)
    d_ffw_in = product(d_gate_low, wg_full, "tf,df->td") + product(d_up_low, wu_full, "tf,df->td")
    d_hidden_part, dg_ffw = norm_backward(hidden_state, ffw_inverse, g_ffw, d_ffw_in)
    d_hidden = grad_output + d_hidden_part
    d_branch, dg_post = norm_backward(branch, post_inverse, g_post, d_hidden)
    d_branch_low = d_branch.astype(low)
    d_branch_low, ffw_got = tie(d_branch_low, ffw_got)
    ffw_sums = links.core_sum(ffw_part, ffw_got)
    ffw_out = links.far_rest(ffw_sums)
    d_branch_low, ffw_out = tie(d_branch_low, ffw_out)
    ffw_got = links.to_far(ffw_out)
    dw_out = product(d_branch_low, attended_low, "td,ta->da")
    d_attended = to_heads(product(d_branch_low, wo_turned, "td,da->ta").astype(low))
    d_heads = d_attended.reshape(n_dp * row_count, head_size)
    delta = jnp.sum(d_heads.astype(f32) * attended, axis=-1)
    d_query, d_mine, d_other = back_keys(
        links, row_count, pieces, query_low, d_heads, log_total, delta, q_pos, q_doc, starts
    )
    d_query, ffw_got = tie(d_query, ffw_got)
    ffw_own, ffw_near = links.far_sum(ffw_sums, ffw_got)
    ffw_got = links.to_near(ffw_near.astype(low))
    d_moving = None
    for mine, other in zip(d_mine, d_other):
        here = mine + other.astype(f32)
        if d_moving is not None:
            here = here + links.down(d_moving.astype(low)).astype(f32)
        d_moving = here
    d_moving, ffw_got = tie(d_moving, ffw_got)
    ffw_share = links.chip_scatter(ffw_own + ffw_got.astype(f32))
    d_value_low = d_moving[:, head_size:].astype(low)
    d_key_normed = rotate(d_moving[:, :head_size], cosine, -sine_part)
    d_key_raw, dg_key = norm_backward(key_raw, key_inverse, g_key, d_key_normed)
    d_key_low = d_key_raw.astype(low)
    d_query_normed = rotate(
        d_query.reshape(n_dp, row_count, head_size), cosine[None], -sine_part[None]
    )
    d_query_raw, dg_query = norm_backward(query_raw, query_inverse, g_query, d_query_normed)
    d_query_low = from_heads(d_query_raw.astype(low))
    d_kv_low = jnp.concatenate(
        links.relative(
            [
                jnp.concatenate(
                    [
                        d_key_low[:, i * cols_k : (i + 1) * cols_k],
                        d_value_low[:, i * cols_k : (i + 1) * cols_k],
                    ],
                    axis=1,
                )
                for i in range(n_dp)
            ]
        ),
        axis=1,
    )
    dw_query = product(normed_low, d_query_low, "td,ta->da")
    dw_kv = product(normed_low, d_kv_low, "td,ta->da")
    d_normed = product(d_query_low, wq_full, "ta,da->td") + product(d_kv_low, wkv_full, "ta,da->td")
    d_stream_part, dg_attn = norm_backward(stream, attn_inverse, g_attn, d_normed)
    grad_tokens = (d_hidden + d_stream_part).astype(low)

    gain_grads = jnp.concatenate(
        [item.reshape(n_dp, -1) for item in (dg_attn, dg_query, dg_key, dg_post, dg_ffw, dg_pffw)],
        axis=1,
    ).reshape(n_dp, gain_used, side)
    gain_grads = jnp.pad(gain_grads, ((0, 0), (0, GAIN_ROWS - gain_used), (0, 0)))
    gain_blocks = links.relative([gain_grads[i] for i in range(n_dp)])
    attn_mine, attn_other = [], []
    for i in range(n_dp):
        left = i * head_size
        middle = left + side
        right = left + head_size
        kv_part = dw_kv[:, i * wide : (i + 1) * wide]
        mine, other = links.swap(
            links.core == 1,
            jnp.concatenate([dw_query[:, left:middle], dw_out[:, left:middle], kv_part[:half]]),
            jnp.concatenate([dw_query[:, middle:right], dw_out[:, middle:right], kv_part[half:]]),
        )
        attn_mine.append(jnp.concatenate([mine, gain_blocks[i]], axis=0))
        attn_other.append(jnp.concatenate([other, gain_blocks[i]], axis=0))
    attn_got = links.to_core(links.core_rest(attn_other))
    attn_sums = links.core_sum(attn_mine, attn_got)
    attn_got = links.to_far(links.far_rest(attn_sums))
    attn_total, attn_near = links.far_sum(attn_sums, attn_got)
    attn_got = links.to_near(attn_near.astype(low))
    attn_got, ffw_share = tie(attn_got, ffw_share)
    ffw_totals = links.chip_gather(ffw_share)
    attn_share = links.chip_scatter(attn_total + attn_got.astype(f32))
    attn_total, attn_rest = links.chip_gather(attn_share)
    ffw_total = links.in_order(ffw_totals[0], ffw_totals[1], 1).astype(f32)
    t_heads = links.in_order(attn_total[:at_kv], attn_rest[:at_kv], 1).astype(f32)
    t_kv = links.in_order(attn_total[at_kv:at_gain], attn_rest[at_kv:at_gain], 0).astype(f32)
    t_gain = attn_total[at_gain : at_gain + gain_used].reshape(-1).astype(f32)
    gain_out = []
    at = 0
    for size in gain_sizes:
        gain_out.append(t_gain[at : at + size])
        at += size
    return (
        (output[None], grad_tokens[None])
        + tuple(gain_out)
        + (
            t_heads[:width],
            t_kv[:, :cols_k],
            t_kv[:, cols_k:],
            jnp.transpose(t_heads[width:]),
            ffw_total[:width],
            ffw_total[width : 2 * width],
            jnp.transpose(ffw_total[2 * width :]),
        )
    )


def solution(mesh):
    placed = (
        P("dp", "ctx", None),
        P("dp", None),
        P("dp"),
        P("dp"),
        P("dp"),
        P("dp"),
        P("dp"),
        P("dp"),
        P(None, "dp"),
        P(None, "dp"),
        P(None, "dp"),
        P("dp", None),
        P(None, "dp"),
        P(None, "dp"),
        P("dp", None),
        P("dp", "ctx", None),
    )
    return jax.shard_map(
        functools.partial(local, n_dp=mesh.shape["dp"], n_ctx=mesh.shape["ctx"]),
        mesh=mesh,
        in_specs=placed,
        out_specs=(
            P("dp", "ctx", None),
            P("dp", "ctx", None),
            P("dp"),
            P("dp"),
            P("dp"),
            P("dp"),
            P("dp"),
            P("dp"),
            P(None, "dp"),
            P(None, "dp"),
            P(None, "dp"),
            P("dp", None),
            P(None, "dp"),
            P(None, "dp"),
            P("dp", None),
        ),
        check_vma=False,
    )
```

```python
import functools
import math

import jax
import jax.numpy as jnp
from jax import lax
from jax.sharding import PartitionSpec as P

EPSILON = 1e-06
THETA = 1000000.0
NEGATIVE = -1e30


def frequencies(head_size):
    half_size = head_size // 2
    return jnp.exp(jnp.arange(half_size, dtype=jnp.float32) * (-2.0 * math.log(THETA) / head_size))


def rotate(value, cosine, sine_part):
    half_size = value.shape[-1] // 2
    leading = value[..., :half_size]
    trailing = value[..., half_size:]
    return jnp.concatenate(
        [leading * cosine - trailing * sine_part, trailing * cosine + leading * sine_part], axis=-1
    )


def doc_info(starts, positions):
    below = starts[None, :] <= positions[:, None]
    doc_ids = jnp.sum(below.astype(jnp.int32), axis=1)
    begins = jnp.max(jnp.where(below, starts[None, :], 0), axis=1)
    return (doc_ids, positions - begins)


def norm_forward(value, gain_vec):
    inverse = lax.rsqrt(jnp.mean(value * value, axis=-1, keepdims=True) + EPSILON)
    return (value * inverse * gain_vec, inverse)


def norm_backward(value, inverse, gain_vec, grad_in):
    scaled = grad_in * gain_vec
    inner_mean = jnp.mean(scaled * value, axis=-1, keepdims=True)
    grad_value = inverse * (scaled - value * inverse * inverse * inner_mean)
    grad_gain = jnp.sum((grad_in * value * inverse).reshape(-1, value.shape[-1]), axis=0)
    return (grad_value, grad_gain)


def product(left, right, form):
    return jnp.einsum(form, left, right, preferred_element_type=jnp.float32)


class Links:
    def __init__(self, n_dp, n_ctx):
        self.n_dp = n_dp
        self.n_ctx = n_ctx
        self.n_chip = n_ctx // 2
        self.dp = lax.axis_index("dp")
        ctx = lax.axis_index("ctx")
        self.core = lax.rem(ctx, 2)
        self.chip = ctx // 2
        self.first = self.core == 0

    def send(self, value, target):
        pairs = []
        for d in range(self.n_dp):
            for c in range(self.n_ctx):
                to_d, to_c = target(d, c)
                if 0 <= to_c < self.n_ctx:
                    pairs.append((d * self.n_ctx + c, to_d * self.n_ctx + to_c))
        return lax.ppermute(value, ("dp", "ctx"), pairs)

    def to_core(self, value):
        return self.send(value, lambda d, c: (d, c ^ 1))

    def to_near(self, value):
        return self.send(value, lambda d, c: (d ^ (1 + c % 2), c))

    def to_far(self, value):
        return self.send(value, lambda d, c: (d ^ (2 - c % 2), c))

    def to_chip(self, value, mask):
        return self.send(value, lambda d, c: (d, c ^ (2 * mask)))

    def up(self, value):
        return self.send(value, lambda d, c: (d, c + 2))

    def down(self, value):
        return self.send(value, lambda d, c: (d, c - 2))

    def swap(self, flag, left, right):
        return (jnp.where(flag, right, left), jnp.where(flag, left, right))

    def in_order(self, mine, other, axis):
        left, right = self.swap(self.core == 1, mine, other)
        return jnp.concatenate([left, right], axis=axis)

    def flip(self, blocks):
        odd, high = (self.dp & 1) == 1, (self.dp & 2) == 2
        b0, b1, b2, b3 = blocks
        b0, b1 = self.swap(odd, b0, b1)
        b2, b3 = self.swap(odd, b2, b3)
        b0, b2 = self.swap(high, b0, b2)
        b1, b3 = self.swap(high, b1, b3)
        return [b0, b1, b2, b3]

    def absolute(self, blocks):
        own, near, far, both = blocks
        near, far = self.swap(self.core == 1, near, far)
        return self.flip([own, near, far, both])

    def relative(self, blocks):
        own, near, far, both = self.flip(blocks)
        near, far = self.swap(self.core == 1, near, far)
        return [own, near, far, both]

    def gather(self, own):
        near = self.to_near(own)
        far = self.to_far(own)
        both = self.to_far(near)
        mine = [own, near, far, both]
        other = [self.to_core(item) for item in (own, far, near, both)]
        return (mine, other)

    def core_rest(self, other):
        return jnp.concatenate([other[i].astype(jnp.bfloat16) for i in (0, 2, 1, 3)], axis=0)

    def core_sum(self, mine, got):
        size = mine[0].shape[0]
        return [
            mine[i] + got[i * size : (i + 1) * size].astype(jnp.float32) for i in range(4)
        ]

    def far_rest(self, sums):
        return jnp.concatenate([item.astype(jnp.bfloat16) for item in sums[2:]], axis=0)

    def far_sum(self, sums, got):
        size = sums[0].shape[0]
        return (
            sums[0] + got[:size].astype(jnp.float32),
            sums[1] + got[size:].astype(jnp.float32),
        )

    def digits(self):
        bits = self.n_chip.bit_length() - 1
        return [(bit, min(2, bits - bit)) for bit in range(0, bits, 2)]

    def chip_scatter(self, total):
        for bit, count in self.digits():
            radix = 1 << count
            digit = (self.chip >> bit) & (radix - 1)
            size = total.shape[0] // radix
            value = lax.dynamic_slice_in_dim(total, digit * size, size, 0)
            for mask in range(1, radix):
                part = lax.dynamic_slice_in_dim(total, (digit ^ mask) * size, size, 0)
                part = self.to_chip(part.astype(jnp.bfloat16), mask << bit)
                value = value + part.astype(jnp.float32)
            total = value
        return total.astype(jnp.bfloat16)

    def chip_gather(self, total):
        for bit, count in reversed(self.digits()):
            radix = 1 << count
            parts = [total] + [self.to_chip(total, mask << bit) for mask in range(1, radix)]
            for place in range(count):
                flag = ((self.chip >> (bit + place)) & 1) == 1
                for i in range(radix):
                    if not i & (1 << place):
                        j = i | (1 << place)
                        parts[i], parts[j] = self.swap(flag, parts[i], parts[j])
            total = jnp.concatenate(parts, axis=0)
        return (total, self.to_core(total))


def tie(*values):
    return lax.optimization_barrier(values)


def key_allowed(links, row_count, at, block, q_pos, q_doc, starts):
    place = at + jnp.arange(block, dtype=jnp.int32)
    step = place // (2 * row_count)
    within = lax.rem(place, 2 * row_count)
    side = within // row_count
    core = jnp.where(side == 0, links.core, 1 - links.core)
    key_pos = ((links.chip - step) * 2 + core) * row_count + lax.rem(within, row_count)
    key_doc, unused_offsets = doc_info(starts, key_pos)
    return (
        (key_pos[None, :] >= 0)
        & (key_pos[None, :] <= q_pos[:, None])
        & (key_doc[None, :] == q_doc[:, None])
    )


def fold_keys(links, row_count, pieces, query, q_pos, q_doc, starts):
    rows, width = query.shape
    factor = 1.0 / math.sqrt(width)
    peak = jnp.full((rows,), NEGATIVE, jnp.float32)
    denominator = jnp.zeros((rows,), jnp.float32)
    accumulated = jnp.zeros((rows, width), jnp.float32)
    at = 0
    for piece in pieces:
        block = piece.shape[0]
        allowed = key_allowed(links, row_count, at, block, q_pos, q_doc, starts)
        at += block
        scores = product(query, piece[:, :width], "re,ke->rk") * factor
        scores = jnp.where(allowed, scores, NEGATIVE)
        peak_new = jnp.maximum(peak, jnp.max(scores, axis=-1))
        weights = jnp.where(allowed, jnp.exp(scores - peak_new[:, None]), 0.0)
        shrink = jnp.exp(peak - peak_new)
        denominator = denominator * shrink + jnp.sum(weights, axis=-1)
        accumulated = accumulated * shrink[:, None] + product(
            weights.astype(jnp.bfloat16), piece[:, width:], "rk,ke->re"
        )
        peak = peak_new
    return (peak, denominator, accumulated)


def back_keys(
    links, row_count, pieces, query, d_heads, log_total, delta, q_pos, q_doc, starts
):
    width = query.shape[1]
    factor = 1.0 / math.sqrt(width)
    d_query = jnp.zeros(query.shape, jnp.float32)
    d_mine, d_other = [], []
    at = sum(piece.shape[0] for piece in pieces)
    for piece in reversed(pieces):
        block = piece.shape[0]
        at -= block
        key_block, value_block = piece[:, :width], piece[:, width:]
        allowed = key_allowed(links, row_count, at, block, q_pos, q_doc, starts)
        scores = product(query, key_block, "re,ke->rk") * factor
        scores = jnp.where(allowed, scores, NEGATIVE)
        probs = jnp.where(allowed, jnp.exp(scores - log_total[:, None]), 0.0)
        d_probs = product(d_heads, value_block, "re,ke->rk")
        d_scores = (probs * (d_probs - delta[:, None])).astype(jnp.bfloat16)
        d_query = d_query + product(d_scores, key_block, "rk,ke->re") * factor
        d_values = product(probs.astype(jnp.bfloat16), d_heads, "rk,re->ke")
        d_keys = product(d_scores, query, "rk,re->ke") * factor
        joined = jnp.concatenate([d_keys, d_values], axis=1)
        joined = joined.reshape(block // (2 * row_count), 2, row_count, 2 * width)
        arrived = links.to_core(joined[:, 1].astype(jnp.bfloat16))
        for step in reversed(range(joined.shape[0])):
            d_mine.append(joined[step, 0])
            d_other.append(arrived[step])
    return (d_query, d_mine, d_other)


GAIN_ROWS = 64


def local(
    tokens,
    doc_starts,
    attn_gain,
    query_gain,
    key_gain,
    post_attn_gain,
    ffw_gain,
    post_ffw_gain,
    w_query,
    w_key,
    w_value,
    w_out,
    w_gate,
    w_up,
    w_down,
    cotangent,
    n_dp,
    n_ctx,
):
    links = Links(n_dp, n_ctx)
    f32 = jnp.float32
    low = jnp.bfloat16
    width = tokens.shape[2]
    gains = (attn_gain, query_gain, key_gain, post_attn_gain, ffw_gain, post_ffw_gain)
    gain_sizes = [item.shape[0] for item in gains]
    cols_k = w_key.shape[1]
    head_size = w_query.shape[1]
    side = head_size // 2
    half = width // 2
    span = w_gate.shape[1] // 2
    at_kv = 2 * width
    at_gain = at_kv + half
    gain_used = sum(gain_sizes) // side

    def core_part(value, axis):
        size = value.shape[axis] // 2
        first = lax.slice_in_dim(value, 0, size, axis=axis)
        second = lax.slice_in_dim(value, size, 2 * size, axis=axis)
        return jnp.where(links.first, first, second)

    gain_block = jnp.concatenate(gains).reshape(gain_used, side)
    gain_block = jnp.pad(gain_block, ((0, GAIN_ROWS - gain_used), (0, 0)))
    attn_own = jnp.concatenate(
        [
            core_part(w_query, 1),
            jnp.transpose(core_part(w_out, 0)),
            core_part(jnp.concatenate([w_key, w_value], axis=1), 0),
            gain_block,
        ],
        axis=0,
    )
    ffw_own = jnp.concatenate(
        [core_part(w_gate, 1), core_part(w_up, 1), jnp.transpose(core_part(w_down, 0))], axis=0
    )
    attn_mine, attn_other = links.gather(attn_own)
    ffw_own, attn_last = tie(ffw_own, attn_mine[3])
    attn_mine[3] = attn_last
    ffw_mine, ffw_other = links.gather(ffw_own)

    gain_all = jnp.stack(
        links.absolute([item[at_gain : at_gain + gain_used] for item in attn_mine])
    ).reshape(n_dp, gain_used * side)
    gain_list = []
    at = 0
    for size in gain_sizes:
        gain_list.append(gain_all[:, at : at + size].reshape(-1).astype(f32))
        at += size
    g_attn, g_query, g_key, g_post, g_ffw, g_pffw = gain_list

    def head_columns(start):
        parts = []
        for mine, other in zip(attn_mine, attn_other):
            parts.extend(
                links.swap(
                    links.core == 1, mine[start : start + width], other[start : start + width]
                )
            )
        return jnp.concatenate(parts, axis=1)

    wq_full = head_columns(0)
    wo_turned = head_columns(width)
    wkv_full = jnp.concatenate(
        [
            links.in_order(mine[at_kv:at_gain], other[at_kv:at_gain], 0)
            for mine, other in zip(attn_mine, attn_other)
        ],
        axis=1,
    )
    ffw_pieces = []
    for mine, other in zip(ffw_mine, ffw_other):
        ffw_pieces.extend((mine, other))

    def ffw_columns(index):
        return jnp.concatenate(
            [item[index * width : (index + 1) * width] for item in ffw_pieces], axis=1
        )

    wg_full, wu_full, wd_turned = [ffw_columns(index) for index in range(3)]

    row_count = tokens.shape[1]
    starts = doc_starts[0]
    positions = lax.axis_index("ctx") * row_count + jnp.arange(row_count, dtype=jnp.int32)
    doc_ids, offsets = doc_info(starts, positions)
    angles = offsets.astype(jnp.float32)[:, None] * frequencies(head_size)[None, :]
    cosine = jnp.cos(angles)
    sine_part = jnp.sin(angles)
    stream = tokens[0].astype(jnp.float32)
    normed, attn_inverse = norm_forward(stream, g_attn)
    normed_low = normed.astype(low)

    def to_heads(value):
        return jnp.stack([value[:, h * head_size : (h + 1) * head_size] for h in range(n_dp)])

    def from_heads(value):
        return jnp.concatenate([value[h] for h in range(n_dp)], axis=1)

    key_value_raw = product(normed_low, wkv_full, "td,da->ta")
    wide = 2 * cols_k
    kv_blocks = links.absolute([key_value_raw[:, i * wide : (i + 1) * wide] for i in range(n_dp)])
    key_raw = jnp.concatenate([item[:, :cols_k] for item in kv_blocks], axis=1)
    value_low = jnp.concatenate([item[:, cols_k:] for item in kv_blocks], axis=1).astype(low)
    key_normed, key_inverse = norm_forward(key_raw, g_key)
    key_low = rotate(key_normed, cosine, sine_part).astype(low)
    moving = jnp.concatenate([key_low, value_low], axis=1)
    pieces = []
    for step in range(links.n_chip):
        pieces.extend((moving, links.to_core(moving)))
        if step + 1 < links.n_chip:
            moving = links.up(moving)
    group = 2 * math.gcd(links.n_chip, 2)
    pieces = [
        jnp.concatenate(pieces[i : i + group], axis=0) for i in range(0, len(pieces), group)
    ]

    query_raw = to_heads(product(normed_low, wq_full, "td,da->ta"))
    query_normed, query_inverse = norm_forward(query_raw, g_query)
    query_low = rotate(query_normed, cosine[None], sine_part[None]).astype(low)
    query_low = query_low.reshape(n_dp * row_count, head_size)
    q_pos = jnp.tile(positions, n_dp)
    q_doc = jnp.tile(doc_ids, n_dp)
    peak, denominator, accumulated = fold_keys(
        links, row_count, pieces, query_low, q_pos, q_doc, starts
    )
    log_total = peak + jnp.log(denominator)
    attended = accumulated / denominator[:, None]
    attended_low = from_heads(attended.astype(low).reshape(n_dp, row_count, head_size))
    branch = product(attended_low, wo_turned, "ta,da->td")
    post_branch, post_inverse = norm_forward(branch, g_post)
    hidden_state = stream + post_branch
    ffw_normed, ffw_inverse = norm_forward(hidden_state, g_ffw)
    ffw_low = ffw_normed.astype(low)
    gate_act = product(ffw_low, wg_full, "td,df->tf")
    up_act = product(ffw_low, wu_full, "td,df->tf")
    inner_act, inner_back = jax.vjp(
        lambda left, right: jax.nn.gelu(left, approximate=True) * right, gate_act, up_act
    )
    inner_low = inner_act.astype(low)
    down_out = product(inner_low, wd_turned, "tf,df->td")
    ffw_branch, down_inverse = norm_forward(down_out, g_pffw)
    output = (hidden_state + ffw_branch).astype(low)
    grad_output = cotangent[0].astype(f32)
    d_down, dg_pffw = norm_backward(down_out, down_inverse, g_pffw, grad_output)
    d_down_low = d_down.astype(low)
    dw_down = product(d_down_low, inner_low, "td,tf->df")
    d_inner = product(d_down_low, wd_turned, "td,df->tf")
    d_gate, d_up = inner_back(tie(d_inner)[0])
    d_gate_low = d_gate.astype(low)
    d_up_low = d_up.astype(low)
    dw_gate = product(ffw_low, d_gate_low, "td,tf->df")
    dw_up = product(ffw_low, d_up_low, "td,tf->df")

    def ffw_grad(index):
        return jnp.concatenate(
            [item[:, index * span : (index + 1) * span] for item in (dw_gate, dw_up, dw_down)],
            axis=0,
        )

    ffw_part = [ffw_grad(2 * i) for i in range(n_dp)]
    ffw_out = links.core_rest([ffw_grad(2 * i + 1) for i in range(n_dp)])
    d_gate_low, d_up_low, ffw_out = tie(d_gate_low, d_up_low, ffw_out)
    ffw_got = links.to_core(ffw_out)
    d_ffw_in = product(d_gate_low, wg_full, "tf,df->td") + product(d_up_low, wu_full, "tf,df->td")
    d_hidden_part, dg_ffw = norm_backward(hidden_state, ffw_inverse, g_ffw, d_ffw_in)
    d_hidden = grad_output + d_hidden_part
    d_branch, dg_post = norm_backward(branch, post_inverse, g_post, d_hidden)
    d_branch_low = d_branch.astype(low)
    d_branch_low, ffw_got = tie(d_branch_low, ffw_got)
    ffw_sums = links.core_sum(ffw_part, ffw_got)
    ffw_out = links.far_rest(ffw_sums)
    d_branch_low, ffw_out = tie(d_branch_low, ffw_out)
    ffw_got = links.to_far(ffw_out)
    dw_out = product(d_branch_low, attended_low, "td,ta->da")
    d_attended = to_heads(product(d_branch_low, wo_turned, "td,da->ta").astype(low))
    d_heads = d_attended.reshape(n_dp * row_count, head_size)
    delta = jnp.sum(d_heads.astype(f32) * attended, axis=-1)
    d_query, d_mine, d_other = back_keys(
        links, row_count, pieces, query_low, d_heads, log_total, delta, q_pos, q_doc, starts
    )
    d_query, ffw_got = tie(d_query, ffw_got)
    ffw_own, ffw_near = links.far_sum(ffw_sums, ffw_got)
    ffw_near = ffw_near.astype(low)
    d_mine[0], ffw_near = tie(d_mine[0], ffw_near)
    ffw_got = links.to_near(ffw_near)
    d_moving = None
    for step, (mine, other) in enumerate(zip(d_mine, d_other)):
        here = mine + other.astype(f32)
        if d_moving is not None:
            here = here + links.down(d_moving.astype(low)).astype(f32)
        d_moving = here
        if step == 1:
            d_moving, ffw_got = tie(d_moving, ffw_got)
    ffw_sum = ffw_own + ffw_got.astype(f32)
    d_moving, ffw_sum = tie(d_moving, ffw_sum)
    ffw_share = links.chip_scatter(ffw_sum)
    d_value_low = d_moving[:, head_size:].astype(low)
    d_key_normed = rotate(d_moving[:, :head_size], cosine, -sine_part)
    d_key_raw, dg_key = norm_backward(key_raw, key_inverse, g_key, d_key_normed)
    d_key_low = d_key_raw.astype(low)
    d_query_normed = rotate(
        d_query.reshape(n_dp, row_count, head_size), cosine[None], -sine_part[None]
    )
    d_query_raw, dg_query = norm_backward(query_raw, query_inverse, g_query, d_query_normed)
    d_query_low = from_heads(d_query_raw.astype(low))
    d_kv_low = jnp.concatenate(
        links.relative(
            [
                jnp.concatenate(
                    [
                        d_key_low[:, i * cols_k : (i + 1) * cols_k],
                        d_value_low[:, i * cols_k : (i + 1) * cols_k],
                    ],
                    axis=1,
                )
                for i in range(n_dp)
            ]
        ),
        axis=1,
    )
    dw_query = product(normed_low, d_query_low, "td,ta->da")
    dw_kv = product(normed_low, d_kv_low, "td,ta->da")
    d_normed = product(d_query_low, wq_full, "ta,da->td") + product(d_kv_low, wkv_full, "ta,da->td")
    d_stream_part, dg_attn = norm_backward(stream, attn_inverse, g_attn, d_normed)
    grad_tokens = (d_hidden + d_stream_part).astype(low)

    gain_grads = jnp.concatenate(
        [item.reshape(n_dp, -1) for item in (dg_attn, dg_query, dg_key, dg_post, dg_ffw, dg_pffw)],
        axis=1,
    ).reshape(n_dp, gain_used, side)
    gain_grads = jnp.pad(gain_grads, ((0, 0), (0, GAIN_ROWS - gain_used), (0, 0)))
    gain_blocks = links.relative([gain_grads[i] for i in range(n_dp)])
    attn_mine, attn_other = [], []
    for i in range(n_dp):
        left = i * head_size
        middle = left + side
        right = left + head_size
        kv_part = dw_kv[:, i * wide : (i + 1) * wide]
        mine, other = links.swap(
            links.core == 1,
            jnp.concatenate([dw_query[:, left:middle], dw_out[:, left:middle], kv_part[:half]]),
            jnp.concatenate([dw_query[:, middle:right], dw_out[:, middle:right], kv_part[half:]]),
        )
        attn_mine.append(jnp.concatenate([mine, gain_blocks[i]], axis=0))
        attn_other.append(jnp.concatenate([other, gain_blocks[i]], axis=0))
    attn_out, ffw_share = tie(links.core_rest(attn_other), ffw_share)
    ffw_totals = links.chip_gather(ffw_share)
    attn_got = links.to_core(attn_out)
    attn_sums = links.core_sum(attn_mine, attn_got)
    attn_got = links.to_far(links.far_rest(attn_sums))
    attn_total, attn_near = links.far_sum(attn_sums, attn_got)
    attn_got = links.to_near(attn_near.astype(low))
    attn_got, *ffw_totals = tie(attn_got, *ffw_totals)
    attn_share = links.chip_scatter(attn_total + attn_got.astype(f32))
    attn_total, attn_rest = links.chip_gather(attn_share)
    ffw_total = links.in_order(ffw_totals[0], ffw_totals[1], 1).astype(f32)
    t_heads = links.in_order(attn_total[:at_kv], attn_rest[:at_kv], 1).astype(f32)
    t_kv = links.in_order(attn_total[at_kv:at_gain], attn_rest[at_kv:at_gain], 0).astype(f32)
    t_gain = attn_total[at_gain : at_gain + gain_used].reshape(-1).astype(f32)
    gain_out = []
    at = 0
    for size in gain_sizes:
        gain_out.append(t_gain[at : at + size])
        at += size
    return (
        (output[None], grad_tokens[None])
        + tuple(gain_out)
        + (
            t_heads[:width],
            t_kv[:, :cols_k],
            t_kv[:, cols_k:],
            jnp.transpose(t_heads[width:]),
            ffw_total[:width],
            ffw_total[width : 2 * width],
            jnp.transpose(ffw_total[2 * width :]),
        )
    )


def solution(mesh):
    placed = (
        P("dp", "ctx", None),
        P("dp", None),
        P("dp"),
        P("dp"),
        P("dp"),
        P("dp"),
        P("dp"),
        P("dp"),
        P(None, "dp"),
        P(None, "dp"),
        P(None, "dp"),
        P("dp", None),
        P(None, "dp"),
        P(None, "dp"),
        P("dp", None),
        P("dp", "ctx", None),
    )
    return jax.shard_map(
        functools.partial(local, n_dp=mesh.shape["dp"], n_ctx=mesh.shape["ctx"]),
        mesh=mesh,
        in_specs=placed,
        out_specs=(
            P("dp", "ctx", None),
            P("dp", "ctx", None),
            P("dp"),
            P("dp"),
            P("dp"),
            P("dp"),
            P("dp"),
            P("dp"),
            P(None, "dp"),
            P(None, "dp"),
            P(None, "dp"),
            P("dp", None),
            P(None, "dp"),
            P(None, "dp"),
            P("dp", None),
        ),
        check_vma=False,
    )
```
